256 devices in a mesh: fsdp: 8 (over x_hi, y), dp: 32 (over x_lo, z, core).
Axes of the slice: x: 4 (x_hi: 2, x_lo: 2; x = x_hi * 2 + x_lo), y: 4, z: 8, core: 2. Of those that a mesh axis runs over, the one named last changes fastest.
Arguments:
- residual: bfloat16 [64, 2048, 8192], P('dp', 'fsdp'), may hold values from -6 to 6
- input_norm_gain: float32 [8192], replicated, may hold values from 0.1 to 1.9
- adapter_entry_matrix: bfloat16 [8192, 128], P('fsdp'), may hold values from -0.0625 to 0.0625
- adapter_exit_matrix: bfloat16 [128, 1024], P(None, 'fsdp'), may hold values from -0.5 to 0.5
- value_output_gradient: bfloat16 [64, 2048, 1024], P('dp', 'fsdp'), may hold values from -6 to 6
- position_example_index: int32 [64, 2048], P('dp', 'fsdp'), may hold values from 0 to 7, never falling along the last dimension, each value on 1 to 1024 neighbouring positions
- live_row_length: int32 [64], P('dp'), may hold values from 256 to 2048, as said below
- random_sketch_keys: int32 [2], replicated, may hold values from 1 to 999999
- reference_gradients: bfloat16 [4096, 8192], P('fsdp', 'dp'), may hold values from -6 to 6
Outputs:
- scores: float32 [512, 4096], P('dp', 'fsdp')
The draws below stay inside these ranges and needn't reach their ends.
Inputs may be any that keep to these rules, and one draw needn't show every extreme that they name: `live_row_length`: positions of a row at or past its length are padding; some row is full. `position_example_index`: within a row the numbers never fall.
All inputs are finite; a program needn't handle non-finite values.
Results may differ from the reference program's by a relative error of at most 0.004.
Values may be sent and summed in bfloat16 or wider, within the bound.
No kernel may reach another device: no remote copies, remote signals or barrier semaphores. Data moves between devices by JAX's collectives and lax.ppermute only.
A program may use at most 128 MiB of HBM per device.

```python
import math
import jax
import jax.numpy as jnp
import numpy as np
from jax import lax

EMBED_SIZE = 8192
VEC_HEAD_SPAN = 1024
ADAPTER_INNER = 128
SKETCH_LAYER_IN1 = 64
SKETCH_THIN_COT2 = 64
SKETCH_THIN_ACT3 = 32
SKETCH_VAL_COT4 = 128
F = 8192
ROW_LEN = 2048
SEQS = 2
EX_ROW = 8
NREF = 4096
ROWS = 64
N_DP = 32


def draw_live_row_length(key, part):
    key = jax.random.fold_in(key, 11)
    first_key, second_key = jax.random.split(key)
    lengths = jax.random.randint(first_key, (ROWS,), ROW_LEN // 8, ROW_LEN + 1, dtype=jnp.int32)
    full_row = jax.random.randint(second_key, (), 0, ROWS, dtype=jnp.int32)
    return jnp.where(jnp.arange(ROWS, dtype=jnp.int32) == full_row, ROW_LEN, lengths).astype(jnp.int32)


def shard_levels(own_key, extent, cuts, smallest, high):
    def one(dim, blocks):
        heights = jax.random.uniform(jax.random.fold_in(jax.random.fold_in(own_key, 6), dim), (blocks,), jnp.float32, smallest / len(cuts), high / len(cuts))
        return jnp.repeat(jnp.exp(heights), extent[dim] // blocks).reshape((-1,) + (1,) * (len(extent) - dim - 1))

    factor_of = one(*cuts[0])
    for cut in cuts[1:]:
        factor_of = factor_of * one(*cut)
    return factor_of


def split_up(number_of, total, reach, skew):
    loads = [(1 << 20) // math.isqrt(grade ** skew) + 1 for grade in range(2, number_of + 1)]
    spare, counts = total - reach - (number_of - 1), [1] * (number_of - 1)
    while spare > 0:
        movable = [i for i in range(number_of - 1) if counts[i] < reach]
        pool, budget = sum([loads[i] for i in movable]), spare
        for i in movable:
            extra = min(reach - counts[i], max(1, budget * loads[i] // pool), spare)
            counts[i] = counts[i] + extra
            spare = spare - extra
    return np.array([reach] + counts)


def ragged_sizes(key, count, total, limit, slope):
    if count == 2:
        one = jax.random.randint(key, (), max(1, total - limit), min(limit, total - 1) + 1)
        return jnp.stack([one, total - one])
    sizes = jnp.asarray(split_up(count, total, limit, slope), jnp.int32)
    pairs = (count - 1) // 2
    giver, receiver = sizes[1:1 + 2 * pairs:2], sizes[2:2 + 2 * pairs:2]
    room = jnp.minimum(giver - 1, limit - receiver)
    passed = jax.random.randint(jax.random.fold_in(key, 1), (pairs,), 0, 1 << 20) % (room + 1)
    sizes = sizes.at[1:1 + 2 * pairs:2].set(giver - passed).at[2:2 + 2 * pairs:2].set(receiver + passed)
    return sizes[jax.random.permutation(jax.random.fold_in(key, 2), count)]


def normal_values(rng, dims, spread, bound, cuts=(), kind=jnp.bfloat16):
    values = spread * jax.random.normal(rng, dims, jnp.float32)
    if cuts:
        values = values * shard_levels(rng, dims, cuts, -0.22, 0.18)
    return jnp.clip(values, -bound, bound).astype(kind)


def setup_inputs(seed: int = 0) -> dict:
    key_of = jax.random.split(jax.random.key(seed), 10)
    return {
        "residual": normal_values(key_of[0], (ROWS, ROW_LEN, EMBED_SIZE), 1.0, 6.0, ((0, 32), (1, 8))),
        "input_norm_gain": jnp.clip(1.0 + 0.18 * jax.random.normal(key_of[1], (EMBED_SIZE,), jnp.float32), 0.1, 1.9),
        "adapter_entry_matrix": normal_values(key_of[2], (EMBED_SIZE, ADAPTER_INNER), EMBED_SIZE ** -0.5, 0.0625, ((0, 8),)),
        "adapter_exit_matrix": normal_values(key_of[3], (ADAPTER_INNER, VEC_HEAD_SPAN), ADAPTER_INNER ** -0.5, 0.5, ((1, 8),)),
        "value_output_gradient": normal_values(key_of[4], (ROWS, ROW_LEN, VEC_HEAD_SPAN), 1.0, 6.0, ((0, 32), (1, 8))),
        "position_example_index": jax.vmap(lambda own: jnp.searchsorted(jnp.cumsum(ragged_sizes(own, EX_ROW, ROW_LEN, ROW_LEN // 2, 2)), jnp.arange(ROW_LEN), side="right"))(jax.random.split(key_of[5], ROWS)).reshape((ROWS, ROW_LEN)).astype(jnp.int32),
        "live_row_length": draw_live_row_length(jax.random.fold_in(key_of[9], 71), 0),
        "random_sketch_keys": jax.random.randint(key_of[7], (2,), 1, 1000000).astype(jnp.int32),
        "reference_gradients": normal_values(key_of[8], (NREF, F), 1.0, 6.0, ((0, 8), (1, 32))),
    }


def plus_minus_lookup(seed_value, table_index, row_count, col_count):
    rows_index = jnp.arange(row_count, dtype=jnp.int32)[:, None]
    cols_index = jnp.arange(col_count, dtype=jnp.int32)[None, :]
    mixed = rows_index * 1103515245 + cols_index * 12345 + seed_value * 69069 + table_index * 362437
    mixed = mixed ^ lax.shift_right_logical(mixed, jnp.int32(15))
    mixed = mixed * 739982445
    mixed = mixed ^ lax.shift_right_logical(mixed, jnp.int32(13))
    low_bit = lax.shift_right_logical(mixed, jnp.int32(9)) & 1
    return (2 * low_bit - 1).astype(jnp.bfloat16)

def rms_norm(flat, input_norm_gain):
    wide = flat.astype(jnp.float32)
    mean_sq = lax.optimization_barrier(jnp.mean(wide * wide, axis=1, keepdims=True))
    return (wide * lax.rsqrt(mean_sq + 1e-05) * input_norm_gain[None, :]).astype(jnp.bfloat16)

def featurize(normed_input, gradient_rows, hidden_state, backward_result, onehot, tables):
    high = lax.Precision.HIGHEST
    first, second, third, fourth = tables
    xs = jnp.dot(normed_input, first, preferred_element_type=jnp.float32) / math.sqrt(normed_input.shape[1])
    gs = jnp.dot(backward_result, second.astype(jnp.float32), precision=high) / math.sqrt(backward_result.shape[1])
    hs = jnp.dot(hidden_state, third.astype(jnp.float32), precision=high) / math.sqrt(hidden_state.shape[1])
    ks = jnp.dot(gradient_rows, fourth, preferred_element_type=jnp.float32) / math.sqrt(gradient_rows.shape[1])
    count = onehot.shape[0]
    examples = onehot.shape[1]
    spread_a = (onehot[:, :, None] * xs[:, None, :]).reshape(count, examples * xs.shape[1])
    part_a = lax.dot_general(spread_a, gs, (((0,), (0,)), ((), ())), precision=high)
    spread_b = (onehot[:, :, None] * hs[:, None, :]).reshape(count, examples * hs.shape[1])
    part_b = lax.dot_general(spread_b, ks, (((0,), (0,)), ((), ())), precision=high)
    return jnp.concatenate([part_a.reshape(examples, -1), part_b.reshape(examples, -1)], axis=1)

def make_tables(random_sketch_keys):
    return (plus_minus_lookup(random_sketch_keys[0], 1, EMBED_SIZE, SKETCH_LAYER_IN1), plus_minus_lookup(random_sketch_keys[0], 2, ADAPTER_INNER, SKETCH_THIN_COT2), plus_minus_lookup(random_sketch_keys[1], 3, ADAPTER_INNER, SKETCH_THIN_ACT3), plus_minus_lookup(random_sketch_keys[1], 4, VEC_HEAD_SPAN, SKETCH_VAL_COT4))

def reference(residual, input_norm_gain, adapter_entry_matrix, adapter_exit_matrix, value_output_gradient, position_example_index, live_row_length, random_sketch_keys, reference_gradients):
    tables = make_tables(random_sketch_keys)
    group_count = SEQS * EX_ROW

    def one_group(group):
        first_row = (group * SEQS).astype(jnp.int32)
        block = lax.dynamic_slice_in_dim(residual, first_row, SEQS, 0).reshape(SEQS * ROW_LEN, EMBED_SIZE)
        gradient_rows = lax.dynamic_slice_in_dim(value_output_gradient, first_row, SEQS, 0).reshape(SEQS * ROW_LEN, VEC_HEAD_SPAN)
        segs = lax.dynamic_slice_in_dim(position_example_index, first_row, SEQS, 0)
        lengths = lax.dynamic_slice_in_dim(live_row_length, first_row, SEQS, 0)
        normed_input = rms_norm(block, input_norm_gain)
        hidden_state = jnp.dot(normed_input, adapter_entry_matrix, preferred_element_type=jnp.float32)
        backward_result = lax.dot_general(gradient_rows, adapter_exit_matrix, (((1,), (1,)), ((), ())), preferred_element_type=jnp.float32)
        positions = jnp.arange(ROW_LEN, dtype=jnp.int32)[None, :]
        live = (positions < lengths[:, None]).reshape(-1)
        example_id = (jnp.arange(SEQS, dtype=jnp.int32)[:, None] * EX_ROW + segs).reshape(-1)
        onehot = ((example_id[:, None] == jnp.arange(group_count, dtype=jnp.int32)[None, :]) & live[:, None]).astype(jnp.float32)
        return featurize(normed_input, gradient_rows, hidden_state, backward_result, onehot, tables)
    features = lax.map(one_group, jnp.arange(N_DP, dtype=jnp.int32)).reshape(N_DP * group_count, -1)
    feat_b = features.astype(jnp.bfloat16)
    feat_wide = feat_b.astype(jnp.float32)
    enorm = lax.rsqrt(lax.optimization_barrier(jnp.sum(feat_wide * feat_wide, axis=1)) + 1e-06)
    ref_wide = reference_gradients.astype(jnp.float32)
    rnorm = lax.rsqrt(lax.optimization_barrier(jnp.sum(ref_wide * ref_wide, axis=1)) + 1e-06)
    dots = lax.dot_general(feat_b, reference_gradients, (((1,), (1,)), ((), ())), preferred_element_type=jnp.float32)
    return dots * enorm[:, None] * rnorm[None, :]
```

```python
import functools
import math

import jax
import jax.numpy as jnp
from jax import lax
from jax.experimental import pallas as pl
from jax.experimental.pallas import tpu as pltpu
from jax.sharding import PartitionSpec as P

BF16, F32, I32 = jnp.bfloat16, jnp.float32, jnp.int32
NT = (((1,), (1,)), ((), ()))
NN = (((1,), (0,)), ((), ()))
MIB = 1024 * 1024


def dot(a, b, dims=NN):
    return lax.dot_general(a, b, dims, preferred_element_type=F32)


def sign_bits(seed, table, row0, rows, cols):
    a = lax.broadcasted_iota(I32, (1, rows), 1) + row0
    b = lax.broadcasted_iota(I32, (cols, 1), 0)
    h = a * 1103515245 + (b * 12345 + (seed * 69069 + table * 362437))
    h = h ^ lax.shift_right_logical(h, jnp.int32(15))
    h = h * 739982445
    h = h ^ lax.shift_right_logical(h, jnp.int32(13))
    return (h & 512) != 0


def signs(seed, table, row0, rows, cols):
    return jnp.where(sign_bits(seed, table, row0, rows, cols), 1.0, -1.0)


def split(v):
    hi = v.astype(BF16)
    return hi, (v - hi.astype(F32)).astype(BF16)


def prep_kernel(me, keys, gain, down, up, out):
    shard = down.shape[0]
    start = pl.multiple_of(me[0] * shard, shard)
    s3 = signs(keys[1], 3, 0, down.shape[1], 32).astype(BF16)
    wb = dot(s3, down[...], NT) * gain[:, pl.ds(start, shard)]
    s2 = signs(keys[0], 2, 0, up.shape[0], 64).astype(BF16)
    hi, lo = split(dot(s2, up[...]))
    wg = jnp.concatenate(
        [w[16 * q : 16 * q + 16] for w in (hi, lo) for q in range(4)], axis=1
    )
    both = jnp.concatenate([wb.astype(BF16), wg], axis=0)
    for n in range(out.shape[0]):
        out[n] = both


def main_kernel(
    me, keys, lengths, x, g, w, gain, index, out, accx, accg, sq, xt, ua, ub
):
    step, steps = pl.program_id(0), pl.num_programs(0)
    chunk, gchunk = x.shape[1], g.shape[1]
    width, gwidth = chunk * steps, gchunk * steps
    tokens = x.shape[0]
    half = tokens // 2

    gain_row = gain[:, pl.ds(pl.multiple_of(step * chunk, chunk), chunk)]
    gain_hi = gain_row.astype(BF16).astype(F32)
    gain_lo = gain_row - gain_hi
    plus = sign_bits(keys[0], 1, step * chunk, chunk, 64)
    w_x = jnp.concatenate(
        [
            jnp.where(plus, gain_hi, -gain_hi).astype(BF16),
            jnp.where(plus, gain_lo, -gain_lo).astype(BF16),
            w[0, 0:32, :],
        ],
        axis=0,
    )
    px = dot(x[...], w_x, NT)
    s4 = signs(keys[1], 4, step * gchunk, gchunk, 128).astype(BF16)
    w_g = jnp.concatenate(
        [w[0, 32:48, 128 * q : 128 * q + 128] for q in range(8)] + [s4], axis=0
    )
    pg = dot(g[...], w_g, NT)
    ps = jnp.zeros((tokens, 128), F32)
    for c in range(chunk // 128):
        piece = x[:, 128 * c : 128 * c + 128].astype(F32)
        ps = ps + piece * piece

    @pl.when(step == 0)
    def _():
        accx[...] = px
        accg[...] = pg
        sq[...] = ps

    @pl.when(step > 0)
    def _():
        accx[...] += px
        accg[...] += pg
        sq[...] += ps

    @pl.when(step == steps - 1)
    def _():
        mean_sq = jnp.sum(sq[...].T, axis=0, keepdims=True) * (1.0 / width)
        r = lax.rsqrt(mean_sq + 1e-05)
        first = accx[:, 0:128].T
        xs = (first[0:64] + first[64:128]) * (r * (1.0 / math.sqrt(width)))
        hs = accx[:, 128:160].T * (r * (1.0 / math.sqrt(128)))
        xh = jnp.concatenate([xs, hs], axis=0)
        hi = xh.astype(BF16).astype(F32)
        xt[0] = hi
        xt[1] = xh - hi

        two = accg[:, 0:128] * (1.0 / math.sqrt(128))
        two = two + pltpu.roll(two, 64, 1)
        row = lax.broadcasted_iota(I32, (tokens, 128), 0) >= half
        lane = lax.broadcasted_iota(I32, (tokens, 128), 1) >= 64
        va_hi, va_lo = split(jnp.where(row == lane, two, 0.0))
        vb_hi, vb_lo = split(accg[:, 128:256] * (1.0 / math.sqrt(gwidth)))

        position = me[0] * half + lax.broadcasted_iota(I32, (8, half), 1)
        example = lax.broadcasted_iota(I32, (8, half), 0)
        m0, m1 = (
            jnp.where(
                (index[n : n + 1, :] == example) & (position < lengths[n]), 1.0, 0.0
            )
            for n in range(2)
        )
        zero = jnp.zeros((8, half), F32)
        m8 = jnp.concatenate([m0, m1], axis=1)
        m16 = jnp.concatenate(
            [
                jnp.concatenate([m0, zero], axis=1),
                jnp.concatenate([zero, m1], axis=1),
            ],
            axis=0,
        )
        for p in range(2):
            for i in range(32):
                ua[p, 16 * i : 16 * i + 16, :] = jnp.concatenate(
                    [
                        xt[p, 2 * i : 2 * i + 1, :] * m8,
                        xt[p, 2 * i + 1 : 2 * i + 2, :] * m8,
                    ],
                    axis=0,
                ).astype(BF16)
                ub[p, 16 * i : 16 * i + 16, :] = (
                    xt[p, 64 + i : 65 + i, :] * m16
                ).astype(BF16)
        fa = dot(ua[0], jnp.concatenate([va_hi, va_lo], axis=1))
        fa = fa[:, 0:128] + fa[:, 128:256] + dot(ua[1], va_hi)
        fb = dot(ub[0], jnp.concatenate([vb_hi, vb_lo], axis=1))
        fb = fb[:, 0:128] + fb[:, 128:256] + dot(ub[1], vb_hi)
        for n in range(8):
            out[n, 0:64, :] = fa[64 * n : 64 * n + 64]
            out[n, 64:128, :] = fb[64 * n : 64 * n + 64]


def sum_kernel(me, parts, own, one, two, three, held):
    total = parts[0]
    for n in range(1, parts.shape[0]):
        total = total + parts[n]
    low = lax.broadcasted_iota(I32, (8, 128), 1) < 64
    for c in range(2):
        lanes = [[], []]
        for i in range(2):
            at = 32 * c + 16 * i
            u, v = total[at : at + 8], total[at + 8 : at + 16]
            lanes[0].append(jnp.where(low, u, pltpu.roll(v, 64, 1)))
            lanes[1].append(jnp.where(low, pltpu.roll(u, 64, 1), v))
        held[c] = jnp.concatenate(
            [jnp.concatenate(p, axis=1) for p in lanes], axis=0
        ).astype(BF16)
        at = 64 + 32 * c
        held[2 + c] = jnp.concatenate(
            [total[at : at + 16], total[at + 16 : at + 32]], axis=1
        ).astype(BF16)
    for k, ref in enumerate((own, one, two, three)):
        ref[...] = held[me[0] ^ k]


def score_kernel(feats, refs, own, one, two, three):
    blocks = feats.shape[0]
    dots = esq = rsq = None
    for n in range(blocks):
        f = feats[n]
        b = refs[:, 256 * n : 256 * n + 256]
        fw, bw = f.astype(F32), b.astype(F32)
        d = dot(f, b, NT)
        e2 = fw * fw
        e2 = e2[:, 0:128] + e2[:, 128:256]
        b2 = bw * bw
        b2 = b2[:, 0:128] + b2[:, 128:256]
        dots = d if dots is None else dots + d
        esq = e2 if esq is None else esq + e2
        rsq = b2 if rsq is None else rsq + b2
    esq = jnp.broadcast_to(jnp.sum(esq, axis=1, keepdims=True), (64, 128))
    rsq = jnp.sum(rsq.T, axis=0, keepdims=True)
    rows = jnp.concatenate(
        [rsq[:, 128 * q : 128 * q + 128] for q in range(4)]
        + [jnp.zeros((12, 128), F32)],
        axis=0,
    )
    for k, ref in enumerate((own, one, two, three)):
        ref[:, 0:512] = dots[16 * k : 16 * k + 16]
        ref[:, 512:640] = esq[16 * k : 16 * k + 16]
        ref[:, 640:768] = rows


def final_kernel(own, one, two, three, out):
    total = (own[...] + one[...]) + (two[...] + three[...])
    enorm = lax.rsqrt(total[:, 512:640] + 1e-06)
    rnorm = lax.rsqrt(total[:, 640:768] + 1e-06)
    for q in range(4):
        out[:, 128 * q : 128 * q + 128] = (
            total[:, 128 * q : 128 * q + 128] * enorm * rnorm[q : q + 1, :]
        )


VMEM = pl.BlockSpec(memory_space=pltpu.VMEM)
SMEM = pl.BlockSpec(memory_space=pltpu.SMEM)


def shape(dims, kind):
    return jax.ShapeDtypeStruct(dims, kind)


def per_device(
    residual,
    input_norm_gain,
    adapter_entry_matrix,
    adapter_exit_matrix,
    value_output_gradient,
    position_example_index,
    live_row_length,
    random_sketch_keys,
    reference_gradients,
):
    seq_count, local_len, width = residual.shape
    tokens = seq_count * local_len
    value_width = value_output_gradient.shape[2]
    n_fsdp, n_dp = lax.axis_size("fsdp"), lax.axis_size("dp")
    fsdp, dp = lax.axis_index("fsdp"), lax.axis_index("dp")
    fsdp_at = fsdp.reshape(1)
    top = n_dp // 2
    four_at = (dp // top * 2 + dp % 2).reshape(1)
    columns = [
        [top * a + 2 * z + c for z in range(top // 2)] for a in range(2) for c in range(2)
    ]
    swaps = [
        [(n, n ^ flip) for n in range(n_dp)] for flip in (1, top, top + 1)
    ]

    refs = lax.all_gather(
        reference_gradients, "dp", axis=1, tiled=True, axis_index_groups=columns
    )

    gain = input_norm_gain.reshape(1, width)
    weights = pl.pallas_call(
        prep_kernel,
        out_shape=shape((n_fsdp, 48, width // n_fsdp), BF16),
        in_specs=[SMEM, SMEM, VMEM, VMEM, VMEM],
        out_specs=VMEM,
        name="prep",
    )(fsdp_at, random_sketch_keys, gain, adapter_entry_matrix, adapter_exit_matrix)
    weights = lax.all_to_all(weights, "fsdp", 0, 0)

    chunk, gchunk = width // n_fsdp, value_width // n_fsdp
    features = pl.pallas_call(
        main_kernel,
        grid=(n_fsdp,),
        out_shape=shape((8, 128, 128), F32),
        in_specs=[
            SMEM,
            SMEM,
            SMEM,
            pl.BlockSpec((tokens, chunk), lambda j: (0, j)),
            pl.BlockSpec((tokens, gchunk), lambda j: (0, j)),
            pl.BlockSpec((1, 48, chunk), lambda j: (j, 0, 0)),
            pl.BlockSpec((1, width), lambda j: (0, 0)),
            pl.BlockSpec((seq_count, local_len), lambda j: (0, 0)),
        ],
        out_specs=pl.BlockSpec((8, 128, 128), lambda j: (0, 0, 0)),
        scratch_shapes=[
            pltpu.VMEM((tokens, 160), F32),
            pltpu.VMEM((tokens, 256), F32),
            pltpu.VMEM((tokens, 128), F32),
            pltpu.VMEM((2, 96, tokens), F32),
            pltpu.VMEM((2, 512, tokens), BF16),
            pltpu.VMEM((2, 512, tokens), BF16),
        ],
        compiler_params=pltpu.CompilerParams(vmem_limit_bytes=24 * MIB),
        name="features",
    )(
        fsdp_at,
        random_sketch_keys,
        live_row_length,
        residual.reshape(tokens, width),
        value_output_gradient.reshape(tokens, value_width),
        weights,
        gain,
        position_example_index,
    )
    features = lax.all_to_all(features, "fsdp", 0, 0)

    pieces = pl.pallas_call(
        sum_kernel,
        out_shape=[shape((16, 256), BF16)] * 4,
        in_specs=[SMEM, VMEM],
        out_specs=[VMEM] * 4,
        scratch_shapes=[pltpu.VMEM((4, 16, 256), BF16)],
        name="sum_features",
    )(four_at, features)
    pieces = [pieces[0]] + [
        lax.ppermute(piece, "dp", swap) for piece, swap in zip(pieces[1:], swaps)
    ]
    feats = jnp.concatenate(pieces, axis=0)
    feats = jnp.broadcast_to(feats[None], (n_fsdp,) + feats.shape)
    feats = lax.all_to_all(feats, "fsdp", 0, 0)

    pieces = pl.pallas_call(
        score_kernel,
        out_shape=[shape((16, 768), F32)] * 4,
        in_specs=[VMEM, VMEM],
        out_specs=[VMEM] * 4,
        compiler_params=pltpu.CompilerParams(vmem_limit_bytes=16 * MIB),
        name="partial_scores",
    )(feats, refs)
    pieces = [pieces[0]] + [
        lax.ppermute(piece, "dp", swap) for piece, swap in zip(pieces[1:], swaps)
    ]
    return pl.pallas_call(
        final_kernel,
        out_shape=shape((16, reference_gradients.shape[0]), F32),
        in_specs=[VMEM] * 4,
        out_specs=VMEM,
        name="scores",
    )(*pieces)


def solution(mesh):
    placed = (
        P("dp", "fsdp", None),
        P(),
        P("fsdp", None),
        P(None, "fsdp"),
        P("dp", "fsdp", None),
        P("dp", "fsdp"),
        P("dp"),
        P(),
        P("fsdp", "dp"),
    )
    return jax.shard_map(
        per_device, mesh=mesh, in_specs=placed, out_specs=P("dp", "fsdp"), check_vma=False
    )
```

```python
import functools
import math

import jax
import jax.numpy as jnp
from jax import lax
from jax.experimental import pallas as pl
from jax.experimental.pallas import tpu as pltpu
from jax.sharding import PartitionSpec as P

BF16, F32, I32 = jnp.bfloat16, jnp.float32, jnp.int32
NT = (((1,), (1,)), ((), ()))
NN = (((1,), (0,)), ((), ()))
MIB = 1024 * 1024
FULL_MIB = 58
AHEAD = 4


def dot(a, b, dims=NN):
    return lax.dot_general(a, b, dims, preferred_element_type=F32)


def sign_bits(seed, table, row0, rows, cols):
    a = lax.broadcasted_iota(I32, (1, rows), 1) + row0
    b = lax.broadcasted_iota(I32, (cols, 1), 0)
    h = a * 1103515245 + (b * 12345 + (seed * 69069 + table * 362437))
    h = h ^ lax.shift_right_logical(h, jnp.int32(15))
    h = h * 739982445
    h = h ^ lax.shift_right_logical(h, jnp.int32(13))
    return (h & 512) != 0


def signs(seed, table, row0, rows, cols):
    return jnp.where(sign_bits(seed, table, row0, rows, cols), 1.0, -1.0)


def split(v):
    hi = v.astype(BF16)
    return hi, (v - hi.astype(F32)).astype(BF16)


def prep_kernel(me, keys, gain, down, up, out):
    shard = down.shape[0]
    start = pl.multiple_of(me[0] * shard, shard)
    s3 = signs(keys[1], 3, 0, down.shape[1], 32).astype(BF16)
    wb = dot(s3, down[...], NT) * gain[:, pl.ds(start, shard)]
    s2 = signs(keys[0], 2, 0, up.shape[0], 64).astype(BF16)
    hi, lo = split(dot(s2, up[...]))
    wg = jnp.concatenate(
        [w[16 * q : 16 * q + 16] for w in (hi, lo) for q in range(4)], axis=1
    )
    both = jnp.concatenate([wb.astype(BF16), wg], axis=0)
    for n in range(out.shape[0]):
        out[n] = both


def copies_of(pairs, sems):
    return [
        pltpu.make_async_copy(a, b, sems.at[n]) for n, (a, b) in enumerate(pairs)
    ]


def x_pieces(x, held):
    steps, _, chunk = held.shape
    return [
        (x.at[:, chunk * n : chunk * n + chunk], held.at[n]) for n in range(steps)
    ]


def early_kernel(
    keys, gain_in, x_in, g_in, xs_out, r_out, ks_out, x, g, gain, table, acc, sq, sems
):
    steps, tokens, chunk = x.shape
    width, gwidth = steps * chunk, g.shape[1]
    copies = copies_of(x_pieces(x_in, x) + [(g_in, g), (gain_in, gain)], sems)
    copies[-1].start()
    for copy in copies[:AHEAD]:
        copy.start()
    s4 = signs(keys[1], 4, 0, gwidth, 128).astype(BF16)
    copies[-1].wait()
    for n in range(steps):
        columns = slice(chunk * n, chunk * n + chunk)
        gain_row = gain[:, columns]
        gain_hi = gain_row.astype(BF16).astype(F32)
        gain_lo = gain_row - gain_hi
        plus = sign_bits(keys[0], 1, n * chunk, chunk, 64)
        table[0:64, columns] = jnp.where(plus, gain_hi, -gain_hi).astype(BF16)
        table[64:128, columns] = jnp.where(plus, gain_lo, -gain_lo).astype(BF16)
    for n in range(0, steps, 2):
        for m in (n, n + 1):
            copies[m].wait()
            if m + AHEAD <= steps:
                copies[m + AHEAD].start()
        px = None
        for m in (n, n + 1):
            p = dot(x[m], table[:, chunk * m : chunk * m + chunk], NT)
            px = p if px is None else px + p
        acc[...] = px if n == 0 else acc[...] + px
        for t in range(0, tokens, 64):
            total = sq[t : t + 64, :] if n else jnp.zeros((64, 128), F32)
            for m in (n, n + 1):
                for c in range(0, chunk, 128):
                    piece = x[m, t : t + 64, c : c + 128].astype(F32)
                    total = total + piece * piece
            sq[t : t + 64, :] = total
    copies[steps].wait()
    ks_out[...] = dot(g[...], s4, NT) * (1.0 / math.sqrt(gwidth))
    mean_sq = jnp.sum(sq[...].T, axis=0, keepdims=True) * (1.0 / width)
    r = lax.rsqrt(mean_sq + 1e-05)
    r_out[...] = jnp.broadcast_to(r, r_out.shape)
    first = acc[...].T
    xs = (first[0:64] + first[64:128]) * (r * (1.0 / math.sqrt(width)))
    hi = xs.astype(BF16).astype(F32)
    xs_out[0] = hi
    xs_out[1] = xs - hi


def main_kernel(
    me, lengths, index_in, xs_in, r_in, ks_in, w_in, g_in, x_in, out_hbm,
    index, xs, r, ks, w, g, x, out, ht, ua, ub, sems, out_sems,
):
    steps, tokens, chunk = x.shape
    half = tokens // 2
    copies = copies_of(
        [(index_in, index), (xs_in, xs), (w_in, w), (g_in, g), (r_in, r), (ks_in, ks)]
        + x_pieces(x_in, x),
        sems,
    )
    for copy in copies[: 6 + AHEAD]:
        copy.start()

    position = me[0] * half + lax.broadcasted_iota(I32, (8, half), 1)
    example = lax.broadcasted_iota(I32, (8, half), 0)
    copies[0].wait()
    m0, m1 = (
        jnp.where(
            (index[n : n + 1, :] == example) & (position < lengths[n]), 1.0, 0.0
        )
        for n in range(2)
    )
    zero = jnp.zeros((8, half), F32)
    m8 = jnp.concatenate([m0, m1], axis=1)
    m16 = jnp.concatenate(
        [jnp.concatenate([m0, zero], axis=1), jnp.concatenate([zero, m1], axis=1)],
        axis=0,
    )
    copies[1].wait()
    for p in range(2):
        for i in range(32):
            ua[p, 16 * i : 16 * i + 16, :] = jnp.concatenate(
                [
                    xs[p, 2 * i : 2 * i + 1, :] * m8,
                    xs[p, 2 * i + 1 : 2 * i + 2, :] * m8,
                ],
                axis=0,
            ).astype(BF16)

    copies[2].wait()
    w_g = jnp.concatenate(
        [
            jnp.concatenate(
                [w[n, 32:48, 128 * q : 128 * q + 128] for q in range(8)], axis=0
            )
            for n in range(steps)
        ],
        axis=1,
    )
    copies[3].wait()
    two = dot(g[...], w_g, NT) * (1.0 / math.sqrt(128))
    two = two + pltpu.roll(two, 64, 1)
    row = lax.broadcasted_iota(I32, (tokens, 128), 0) >= half
    lane = lax.broadcasted_iota(I32, (tokens, 128), 1) >= 64
    va = jnp.concatenate(split(jnp.where(row == lane, two, 0.0)), axis=1)
    fa = dot(ua[0], va)
    fa = fa[:, 0:128] + fa[:, 128:256] + dot(ua[1], va[:, 0:128])
    for n in range(8):
        out[n, 0:64, :] = fa[64 * n : 64 * n + 64]
    copies[4].wait()
    copies[5].wait()
    vb = jnp.concatenate(split(ks[...]), axis=1)

    acc = None
    for n in range(steps):
        copies[6 + n].wait()
        if n + AHEAD < steps:
            copies[6 + n + AHEAD].start()
        p = dot(w[n, 0:32, :], x[n], NT)
        acc = p if acc is None else acc + p
    hs = acc * (r[0:1, :] * (1.0 / math.sqrt(128)))
    hi = hs.astype(BF16).astype(F32)
    ht[0] = hi
    ht[1] = hs - hi
    for p in range(2):
        for i in range(32):
            ub[p, 16 * i : 16 * i + 16, :] = (ht[p, i : i + 1, :] * m16).astype(BF16)
    fb = dot(ub[0], vb)
    fb = fb[:, 0:128] + fb[:, 128:256] + dot(ub[1], vb[:, 0:128])
    for n in range(8):
        out[n, 64:128, :] = fb[64 * n : 64 * n + 64]
    done = pltpu.make_async_copy(out, out_hbm, out_sems.at[0])
    done.start()
    done.wait()


def sum_kernel(me, parts, own, one, two, three, held):
    total = parts[0]
    for n in range(1, parts.shape[0]):
        total = total + parts[n]
    low = lax.broadcasted_iota(I32, (8, 128), 1) < 64
    for c in range(2):
        lanes = [[], []]
        for i in range(2):
            at = 32 * c + 16 * i
            u, v = total[at : at + 8], total[at + 8 : at + 16]
            lanes[0].append(jnp.where(low, u, pltpu.roll(v, 64, 1)))
            lanes[1].append(jnp.where(low, pltpu.roll(u, 64, 1), v))
        held[c] = jnp.concatenate(
            [jnp.concatenate(p, axis=1) for p in lanes], axis=0
        ).astype(BF16)
        at = 64 + 32 * c
        held[2 + c] = jnp.concatenate(
            [total[at : at + 16], total[at + 16 : at + 32]], axis=1
        ).astype(BF16)
    for k, ref in enumerate((own, one, two, three)):
        ref[...] = held[me[0] ^ k]


def score_kernel(at, feats, *rest):
    refs, (own, one, two, three) = rest[:-4], rest[-4:]
    dots = esq = rsq = None
    for k, ref in enumerate(refs):
        f, b = feats[(at[0] + 8 - k) & 7], ref[...]
        fw, bw = f.astype(F32), b.astype(F32)
        d = dot(f, b, NT)
        e2 = fw * fw
        e2 = e2[:, 0:128] + e2[:, 128:256]
        b2 = bw * bw
        b2 = b2[:, 0:128] + b2[:, 128:256]
        dots = d if dots is None else dots + d
        esq = e2 if esq is None else esq + e2
        rsq = b2 if rsq is None else rsq + b2
    esq = jnp.broadcast_to(jnp.sum(esq, axis=1, keepdims=True), (64, 128))
    rsq = jnp.sum(rsq.T, axis=0, keepdims=True)
    rows = jnp.concatenate(
        [rsq[:, 128 * q : 128 * q + 128] for q in range(4)]
        + [jnp.zeros((12, 128), F32)],
        axis=0,
    )
    for k, ref in enumerate((own, one, two, three)):
        ref[:, 0:512] = dots[16 * k : 16 * k + 16]
        ref[:, 512:640] = esq[16 * k : 16 * k + 16]
        ref[:, 640:768] = rows


def final_kernel(own, one, two, three, out):
    total = (own[...] + one[...]) + (two[...] + three[...])
    enorm = lax.rsqrt(total[:, 512:640] + 1e-06)
    rnorm = lax.rsqrt(total[:, 640:768] + 1e-06)
    for q in range(4):
        out[:, 128 * q : 128 * q + 128] = (
            total[:, 128 * q : 128 * q + 128] * enorm * rnorm[q : q + 1, :]
        )


VMEM = pl.BlockSpec(memory_space=pltpu.VMEM)
SMEM = pl.BlockSpec(memory_space=pltpu.SMEM)
HBM = pl.BlockSpec(memory_space=pltpu.HBM)


def shape(dims, kind):
    return jax.ShapeDtypeStruct(dims, kind)


def kernel(body, name, out, ins, scratch=(), vmem=4, flops=0, nbytes=0, outs=VMEM):
    single = not isinstance(out, list)
    return pl.pallas_call(
        body,
        out_shape=out,
        in_specs=ins,
        out_specs=outs if single else [outs] * len(out),
        scratch_shapes=scratch,
        compiler_params=pltpu.CompilerParams(vmem_limit_bytes=vmem * MIB),
        cost_estimate=pl.CostEstimate(flops=flops, bytes_accessed=nbytes, transcendentals=0),
        name=name,
    )


def per_device(
    residual,
    input_norm_gain,
    adapter_entry_matrix,
    adapter_exit_matrix,
    value_output_gradient,
    position_example_index,
    live_row_length,
    random_sketch_keys,
    reference_gradients,
):
    seq_count, local_len, width = residual.shape
    tokens = seq_count * local_len
    value_width = value_output_gradient.shape[2]
    n_fsdp, n_dp = lax.axis_size("fsdp"), lax.axis_size("dp")
    fsdp, dp = lax.axis_index("fsdp"), lax.axis_index("dp")
    top = n_dp // 2
    fsdp_at = fsdp.reshape(1)
    z_at = (dp // 2 % (top // 2)).reshape(1)
    four_at = (dp // top * 2 + dp % 2).reshape(1)
    swaps = [[(n, n ^ flip) for n in range(n_dp)] for flip in (1, top, top + 1)]
    up, down = (
        [(n, n // top * top + (n + 2 * way) % top) for n in range(n_dp)] for way in (1, -1)
    )
    tie = lax.optimization_barrier

    x = residual.reshape(tokens, width)
    g = value_output_gradient.reshape(tokens, value_width)
    gain = input_norm_gain.reshape(1, width)
    chunk = width // n_fsdp

    refs_up = [lax.ppermute(reference_gradients, "dp", up)]
    refs_down = [lax.ppermute(reference_gradients, "dp", down)]

    weights = kernel(
        prep_kernel,
        "prep",
        shape((n_fsdp, 48, chunk), BF16),
        [SMEM, SMEM, VMEM, VMEM, VMEM],
        vmem=FULL_MIB,
    )(fsdp_at, random_sketch_keys, gain, adapter_entry_matrix, adapter_exit_matrix)
    weights = lax.all_to_all(weights, "fsdp", 0, 0)

    held = [
        pltpu.VMEM((n_fsdp, tokens, chunk), BF16),
        pltpu.VMEM((tokens, value_width), BF16),
    ]
    early = kernel(
        early_kernel,
        "early",
        [
            shape((2, 64, tokens), F32),
            shape((8, tokens), F32),
            shape((tokens, 128), F32),
        ],
        [SMEM] + [HBM] * 3,
        held
        + [
            pltpu.VMEM((1, width), F32),
            pltpu.VMEM((128, width), BF16),
            pltpu.VMEM((tokens, 128), F32),
            pltpu.VMEM((tokens, 128), F32),
            pltpu.SemaphoreType.DMA((2 + n_fsdp,)),
        ],
        vmem=FULL_MIB,
        flops=2 * tokens * width * 256,
        nbytes=12 * MIB,
    )(random_sketch_keys, gain, x, g)
    early, refs_up[0], refs_down[0] = tie((early, refs_up[0], refs_down[0]))
    refs_up.append(lax.ppermute(refs_up[0], "dp", up))
    refs_down.append(lax.ppermute(refs_down[0], "dp", down))

    features = kernel(
        main_kernel,
        "features",
        shape((8, 128, 128), F32),
        [SMEM] * 2 + [HBM] * 7,
        [
            pltpu.VMEM((seq_count, local_len), I32),
            pltpu.VMEM((2, 64, tokens), F32),
            pltpu.VMEM((8, tokens), F32),
            pltpu.VMEM((tokens, 128), F32),
            pltpu.VMEM((n_fsdp, 48, chunk), BF16),
            held[1],
            held[0],
            pltpu.VMEM((8, 128, 128), F32),
            pltpu.VMEM((2, 32, tokens), F32),
            pltpu.VMEM((2, 512, tokens), BF16),
            pltpu.VMEM((2, 512, tokens), BF16),
            pltpu.SemaphoreType.DMA((6 + n_fsdp,)),
            pltpu.SemaphoreType.DMA((1,)),
        ],
        vmem=FULL_MIB,
        flops=2 * tokens * width * 256,
        nbytes=12 * MIB,
        outs=HBM,
    )(fsdp_at, live_row_length, position_example_index, *early, weights, g, x)
    features, refs_up[1], refs_down[1] = tie((features, refs_up[1], refs_down[1]))
    refs_up.append(lax.ppermute(refs_up[1], "dp", up))
    refs_down.append(lax.ppermute(refs_down[1], "dp", down))
    features = lax.all_to_all(features, "fsdp", 0, 0)

    pieces = kernel(
        sum_kernel,
        "sum_features",
        [shape((16, 256), BF16)] * 4,
        [SMEM, VMEM],
        [pltpu.VMEM((4, 16, 256), BF16)],
    )(four_at, features)
    pieces = [pieces[0]] + [
        lax.ppermute(piece, "dp", swap) for piece, swap in zip(pieces[1:], swaps)
    ]
    feats = jnp.concatenate(pieces, axis=0)
    feats, refs_up[2], refs_down[2] = tie((feats, refs_up[2], refs_down[2]))
    refs_up.append(lax.ppermute(refs_up[2], "dp", up))
    feats = jnp.broadcast_to(feats[None], (n_fsdp,) + feats.shape)
    feats = lax.all_to_all(feats, "fsdp", 0, 0)

    refs = [reference_gradients] + refs_up + refs_down[::-1]
    pieces = kernel(
        score_kernel,
        "partial_scores",
        [shape((16, 768), F32)] * 4,
        [SMEM] + [VMEM] * 9,
        vmem=8,
    )(z_at, feats, *refs)
    pieces = [pieces[0]] + [
        lax.ppermute(piece, "dp", swap) for piece, swap in zip(pieces[1:], swaps)
    ]
    return kernel(
        final_kernel,
        "scores",
        shape((16, reference_gradients.shape[0]), F32),
        [VMEM] * 4,
    )(*pieces)


def solution(mesh):
    placed = (
        P("dp", "fsdp", None),
        P(),
        P("fsdp", None),
        P(None, "fsdp"),
        P("dp", "fsdp", None),
        P("dp", "fsdp"),
        P("dp"),
        P(),
        P("fsdp", "dp"),
    )
    return jax.shard_map(
        per_device, mesh=mesh, in_specs=placed, out_specs=P("dp", "fsdp"), check_vma=False
    )
```

```python
import functools
import math

import jax
import jax.numpy as jnp
from jax import lax
from jax.experimental import pallas as pl
from jax.experimental.pallas import tpu as pltpu
from jax.sharding import PartitionSpec as P

BF16, F32, I32 = jnp.bfloat16, jnp.float32, jnp.int32
NT = (((1,), (1,)), ((), ()))
NN = (((1,), (0,)), ((), ()))
MIB = 1024 * 1024
FULL_MIB = 58


def dot(a, b, dims=NN):
    return lax.dot_general(a, b, dims, preferred_element_type=F32)


def sign_bits(seed, table, row0, rows, cols):
    a = lax.broadcasted_iota(I32, (1, rows), 1) + row0
    b = lax.broadcasted_iota(I32, (cols, 1), 0)
    h = a * 1103515245 + (b * 12345 + (seed * 69069 + table * 362437))
    h = h ^ lax.shift_right_logical(h, jnp.int32(15))
    h = h * 739982445
    h = h ^ lax.shift_right_logical(h, jnp.int32(13))
    return (h & 512) != 0


def signs(seed, table, row0, rows, cols):
    return jnp.where(sign_bits(seed, table, row0, rows, cols), 1.0, -1.0)


def split(v):
    hi = v.astype(BF16)
    return hi, (v - hi.astype(F32)).astype(BF16)


def prep_kernel(me, keys, gain, down, up, out):
    shard = down.shape[0]
    rows = shard // 128
    own_gain = gain[pl.ds(pl.multiple_of(me[0] * rows, rows), rows), :]
    s3 = signs(keys[1], 3, 0, down.shape[1], 32).astype(BF16)
    wb = dot(s3, down[...], NT)
    wb = jnp.concatenate(
        [wb[:, 128 * q : 128 * q + 128] * own_gain[q : q + 1, :] for q in range(rows)],
        axis=1,
    )
    s2 = signs(keys[0], 2, 0, up.shape[0], 64).astype(BF16)
    hi, lo = split(dot(s2, up[...]))
    wg = jnp.concatenate(
        [w[16 * q : 16 * q + 16] for w in (hi, lo) for q in range(4)], axis=1
    )
    both = jnp.concatenate([wb.astype(BF16), wg], axis=0)
    for n in range(out.shape[0]):
        out[n] = both


def copies_of(pairs, sems):
    return [
        pltpu.make_async_copy(a, b, sems.at[n]) for n, (a, b) in enumerate(pairs)
    ]


def x_pieces(x, held):
    steps, _, chunk = held.shape
    return [
        (x.at[:, chunk * n : chunk * n + chunk], held.at[n]) for n in range(steps)
    ]


def early_kernel(
    keys, gain_in, x_in, g_in, xs_out, r_out, ks_out, x, g, gain, table, acc, sq, sems
):
    steps, tokens, chunk = x.shape
    width, gwidth = steps * chunk, g.shape[1]
    copies = copies_of(x_pieces(x_in, x) + [(g_in, g), (gain_in, gain)], sems)
    copies[-1].start()
    for copy in copies[:-1]:
        copy.start()
    s4 = signs(keys[1], 4, 0, gwidth, 128).astype(BF16)
    copies[-1].wait()
    for n in range(0, width, 128):
        gain_row = gain[n // 128 : n // 128 + 1, :]
        gain_hi = gain_row.astype(BF16).astype(F32)
        gain_lo = gain_row - gain_hi
        plus = sign_bits(keys[0], 1, n, 128, 64)
        table[0:64, n : n + 128] = jnp.where(plus, gain_hi, -gain_hi).astype(BF16)
        table[64:128, n : n + 128] = jnp.where(plus, gain_lo, -gain_lo).astype(BF16)
    acc[...] = jnp.zeros_like(acc)
    sq[...] = jnp.zeros_like(sq)
    @pl.loop(0, steps // 2)
    def _(pair):
        both = [2 * pair, 2 * pair + 1]
        columns = [pl.ds(pl.multiple_of(n * chunk, chunk), chunk) for n in both]
        for n, c in zip(both, columns):
            pltpu.make_async_copy(x_in.at[:, c], x.at[n], sems.at[n]).wait()
        acc[...] += dot(x[both[0]], table[:, columns[0]], NT) + dot(
            x[both[1]], table[:, columns[1]], NT
        )
        for t in range(0, tokens, 64):
            total = sq[t : t + 64, :]
            for n in both:
                for c in range(0, chunk, 128):
                    piece = x[n, t : t + 64, c : c + 128].astype(F32)
                    total = total + piece * piece
            sq[t : t + 64, :] = total

    copies[steps].wait()
    ks_out[...] = dot(g[...], s4, NT) * (1.0 / math.sqrt(gwidth))
    mean_sq = jnp.sum(sq[...].T, axis=0, keepdims=True) * (1.0 / width)
    r = lax.rsqrt(mean_sq + 1e-05)
    r_out[...] = jnp.broadcast_to(r, r_out.shape)
    first = acc[...].T
    xs = (first[0:64] + first[64:128]) * (r * (1.0 / math.sqrt(width)))
    hi = xs.astype(BF16).astype(F32)
    xs_out[0] = hi
    xs_out[1] = xs - hi


def main_kernel(
    me, lengths, index_in, xs_in, r_in, ks_in, w_in, g_in, x_in, out_hbm,
    index, xs, r, ks, w, g, x, out, ht, ua, ub, sems, out_sems,
):
    steps, tokens, chunk = x.shape
    half = tokens // 2
    copies = copies_of(
        [(index_in, index), (xs_in, xs), (w_in, w), (g_in, g), (r_in, r), (ks_in, ks)]
        + x_pieces(x_in, x),
        sems,
    )
    for copy in copies:
        copy.start()

    position = me[0] * half + lax.broadcasted_iota(I32, (8, half), 1)
    example = lax.broadcasted_iota(I32, (8, half), 0)
    copies[0].wait()
    m0, m1 = (
        jnp.where(
            (index[n : n + 1, :] == example) & (position < lengths[n]), 1.0, 0.0
        )
        for n in range(2)
    )
    zero = jnp.zeros((8, half), F32)
    m8 = jnp.concatenate([m0, m1], axis=1)
    m16 = jnp.concatenate(
        [jnp.concatenate([m0, zero], axis=1), jnp.concatenate([zero, m1], axis=1)],
        axis=0,
    )
    copies[1].wait()
    for p in range(2):
        for i in range(32):
            ua[p, 16 * i : 16 * i + 16, :] = jnp.concatenate(
                [
                    xs[p, 2 * i : 2 * i + 1, :] * m8,
                    xs[p, 2 * i + 1 : 2 * i + 2, :] * m8,
                ],
                axis=0,
            ).astype(BF16)

    copies[2].wait()
    w_g = jnp.concatenate(
        [
            jnp.concatenate(
                [w[n, 32:48, 128 * q : 128 * q + 128] for q in range(8)], axis=0
            )
            for n in range(steps)
        ],
        axis=1,
    )
    copies[3].wait()
    two = dot(g[...], w_g, NT) * (1.0 / math.sqrt(128))
    two = two + pltpu.roll(two, 64, 1)
    row = lax.broadcasted_iota(I32, (tokens, 128), 0) >= half
    lane = lax.broadcasted_iota(I32, (tokens, 128), 1) >= 64
    va = jnp.concatenate(split(jnp.where(row == lane, two, 0.0)), axis=1)
    fa = dot(ua[0], va)
    fa = fa[:, 0:128] + fa[:, 128:256] + dot(ua[1], va[:, 0:128])
    for n in range(8):
        out[n, 0:64, :] = fa[64 * n : 64 * n + 64]
    done = [
        pltpu.make_async_copy(
            out.at[:, 64 * n : 64 * n + 64], out_hbm.at[:, 64 * n : 64 * n + 64], out_sems.at[n]
        )
        for n in range(2)
    ]
    done[0].start()
    copies[4].wait()
    copies[5].wait()
    vb = jnp.concatenate(split(ks[...]), axis=1)

    acc = None
    for n in range(steps):
        copies[6 + n].wait()
        p = dot(w[n, 0:32, :], x[n], NT)
        acc = p if acc is None else acc + p
    hs = acc * (r[0:1, :] * (1.0 / math.sqrt(128)))
    hi = hs.astype(BF16).astype(F32)
    ht[0] = hi
    ht[1] = hs - hi
    for p in range(2):
        for i in range(32):
            ub[p, 16 * i : 16 * i + 16, :] = (ht[p, i : i + 1, :] * m16).astype(BF16)
    fb = dot(ub[0], vb)
    fb = fb[:, 0:128] + fb[:, 128:256] + dot(ub[1], vb[:, 0:128])
    for n in range(8):
        out[n, 64:128, :] = fb[64 * n : 64 * n + 64]
    done[1].start()
    for copy in done:
        copy.wait()


def sum_kernel(me, parts, own, one, two, three, held):
    total = parts[0]
    for n in range(1, parts.shape[0]):
        total = total + parts[n]
    low = lax.broadcasted_iota(I32, (8, 128), 1) < 64
    for c in range(2):
        lanes = [[], []]
        for i in range(2):
            at = 32 * c + 16 * i
            u, v = total[at : at + 8], total[at + 8 : at + 16]
            lanes[0].append(jnp.where(low, u, pltpu.roll(v, 64, 1)))
            lanes[1].append(jnp.where(low, pltpu.roll(u, 64, 1), v))
        held[c] = jnp.concatenate(
            [jnp.concatenate(p, axis=1) for p in lanes], axis=0
        ).astype(BF16)
        at = 64 + 32 * c
        held[2 + c] = jnp.concatenate(
            [total[at : at + 16], total[at + 16 : at + 32]], axis=1
        ).astype(BF16)
    for k, ref in enumerate((own, one, two, three)):
        ref[...] = held[me[0] ^ k]


def score_kernel(at, feats, *rest):
    refs, (own, one, two, three) = rest[:-4], rest[-4:]
    dots = esq = rsq = None
    for k, ref in enumerate(refs):
        f, b = feats[(at[0] + 8 - k) & 7], ref[...]
        fw, bw = f.astype(F32), b.astype(F32)
        d = dot(f, b, NT)
        e2 = fw * fw
        e2 = e2[:, 0:128] + e2[:, 128:256]
        b2 = bw * bw
        b2 = b2[:, 0:128] + b2[:, 128:256]
        dots = d if dots is None else dots + d
        esq = e2 if esq is None else esq + e2
        rsq = b2 if rsq is None else rsq + b2
    esq = jnp.broadcast_to(jnp.sum(esq, axis=1, keepdims=True), (64, 128))
    rsq = jnp.sum(rsq.T, axis=0, keepdims=True)
    rows = jnp.concatenate(
        [rsq[:, 128 * q : 128 * q + 128] for q in range(4)]
        + [jnp.zeros((12, 128), F32)],
        axis=0,
    )
    for k, ref in enumerate((own, one, two, three)):
        ref[:, 0:512] = dots[16 * k : 16 * k + 16]
        ref[:, 512:640] = esq[16 * k : 16 * k + 16]
        ref[:, 640:768] = rows


def final_kernel(own, one, two, three, out):
    total = (own[...] + one[...]) + (two[...] + three[...])
    enorm = lax.rsqrt(total[:, 512:640] + 1e-06)
    rnorm = lax.rsqrt(total[:, 640:768] + 1e-06)
    for q in range(4):
        out[:, 128 * q : 128 * q + 128] = (
            total[:, 128 * q : 128 * q + 128] * enorm * rnorm[q : q + 1, :]
        )


VMEM = pl.BlockSpec(memory_space=pltpu.VMEM)
SMEM = pl.BlockSpec(memory_space=pltpu.SMEM)
HBM = pl.BlockSpec(memory_space=pltpu.HBM)


def shape(dims, kind):
    return jax.ShapeDtypeStruct(dims, kind)


def kernel(body, name, out, ins, scratch=(), vmem=4, flops=0, nbytes=0, outs=VMEM):
    single = not isinstance(out, list)
    return pl.pallas_call(
        body,
        out_shape=out,
        in_specs=ins,
        out_specs=outs if single else [outs] * len(out),
        scratch_shapes=scratch,
        compiler_params=pltpu.CompilerParams(vmem_limit_bytes=vmem * MIB),
        cost_estimate=pl.CostEstimate(flops=flops, bytes_accessed=nbytes, transcendentals=0),
        name=name,
    )


def per_device(
    residual,
    input_norm_gain,
    adapter_entry_matrix,
    adapter_exit_matrix,
    value_output_gradient,
    position_example_index,
    live_row_length,
    random_sketch_keys,
    reference_gradients,
):
    seq_count, local_len, width = residual.shape
    tokens = seq_count * local_len
    value_width = value_output_gradient.shape[2]
    n_fsdp, n_dp = lax.axis_size("fsdp"), lax.axis_size("dp")
    fsdp, dp = lax.axis_index("fsdp"), lax.axis_index("dp")
    top = n_dp // 2
    fsdp_at = fsdp.reshape(1)
    z_at = (dp // 2 % (top // 2)).reshape(1)
    four_at = (dp // top * 2 + dp % 2).reshape(1)
    swaps = [[(n, n ^ flip) for n in range(n_dp)] for flip in (1, top, top + 1)]
    up, down = (
        [(n, n // top * top + (n + 2 * way) % top) for n in range(n_dp)] for way in (1, -1)
    )
    tie = lax.optimization_barrier

    x = residual.reshape(tokens, width)
    g = value_output_gradient.reshape(tokens, value_width)
    gain = input_norm_gain.reshape(width // 128, 128)
    chunk = width // n_fsdp

    refs_up = [lax.ppermute(reference_gradients, "dp", up)]
    refs_down = [lax.ppermute(reference_gradients, "dp", down)]

    weights = kernel(
        prep_kernel,
        "prep",
        shape((n_fsdp, 48, chunk), BF16),
        [SMEM, SMEM, VMEM, VMEM, VMEM],
        vmem=FULL_MIB,
    )(fsdp_at, random_sketch_keys, gain, adapter_entry_matrix, adapter_exit_matrix)
    weights = lax.all_to_all(weights, "fsdp", 0, 0)

    held = [
        pltpu.VMEM((n_fsdp, tokens, chunk), BF16),
        pltpu.VMEM((tokens, value_width), BF16),
    ]
    early = kernel(
        early_kernel,
        "early",
        [
            shape((2, 64, tokens), F32),
            shape((8, tokens), F32),
            shape((tokens, 128), F32),
        ],
        [SMEM] + [HBM] * 3,
        held
        + [
            pltpu.VMEM((width // 128, 128), F32),
            pltpu.VMEM((128, width), BF16),
            pltpu.VMEM((tokens, 128), F32),
            pltpu.VMEM((tokens, 128), F32),
            pltpu.SemaphoreType.DMA((2 + n_fsdp,)),
        ],
        vmem=FULL_MIB,
        flops=2 * tokens * width * 256,
        nbytes=12 * MIB,
    )(random_sketch_keys, gain, x, g)
    early, refs_up[0], refs_down[0] = tie((early, refs_up[0], refs_down[0]))
    refs_up.append(lax.ppermute(refs_up[0], "dp", up))
    refs_down.append(lax.ppermute(refs_down[0], "dp", down))

    features = kernel(
        main_kernel,
        "features",
        shape((8, 128, 128), F32),
        [SMEM] * 2 + [HBM] * 7,
        [
            pltpu.VMEM((seq_count, local_len), I32),
            pltpu.VMEM((2, 64, tokens), F32),
            pltpu.VMEM((8, tokens), F32),
            pltpu.VMEM((tokens, 128), F32),
            pltpu.VMEM((n_fsdp, 48, chunk), BF16),
            held[1],
            held[0],
            pltpu.VMEM((8, 128, 128), F32),
            pltpu.VMEM((2, 32, tokens), F32),
            pltpu.VMEM((2, 512, tokens), BF16),
            pltpu.VMEM((2, 512, tokens), BF16),
            pltpu.SemaphoreType.DMA((6 + n_fsdp,)),
            pltpu.SemaphoreType.DMA((2,)),
        ],
        vmem=FULL_MIB,
        flops=2 * tokens * width * 256,
        nbytes=12 * MIB,
        outs=HBM,
    )(fsdp_at, live_row_length, position_example_index, *early, weights, g, x)
    features, refs_up[1], refs_down[1] = tie((features, refs_up[1], refs_down[1]))
    refs_up.append(lax.ppermute(refs_up[1], "dp", up))
    refs_down.append(lax.ppermute(refs_down[1], "dp", down))
    features = lax.all_to_all(features, "fsdp", 0, 0)

    pieces = kernel(
        sum_kernel,
        "sum_features",
        [shape((16, 256), BF16)] * 4,
        [SMEM, VMEM],
        [pltpu.VMEM((4, 16, 256), BF16)],
    )(four_at, features)
    pieces = [pieces[0]] + [
        lax.ppermute(piece, "dp", swap) for piece, swap in zip(pieces[1:], swaps)
    ]
    feats = jnp.concatenate(pieces, axis=0)
    feats, refs_up[2], refs_down[2] = tie((feats, refs_up[2], refs_down[2]))
    refs_up.append(lax.ppermute(refs_up[2], "dp", up))
    feats = jnp.broadcast_to(feats[None], (n_fsdp,) + feats.shape)
    feats = lax.all_to_all(feats, "fsdp", 0, 0)

    refs = [reference_gradients] + refs_up + refs_down[::-1]
    pieces = kernel(
        score_kernel,
        "partial_scores",
        [shape((16, 768), F32)] * 4,
        [SMEM] + [VMEM] * 9,
        vmem=8,
    )(z_at, feats, *refs)
    pieces = [pieces[0]] + [
        lax.ppermute(piece, "dp", swap) for piece, swap in zip(pieces[1:], swaps)
    ]
    return kernel(
        final_kernel,
        "scores",
        shape((16, reference_gradients.shape[0]), F32),
        [VMEM] * 4,
    )(*pieces)


def solution(mesh):
    placed = (
        P("dp", "fsdp", None),
        P(),
        P("fsdp", None),
        P(None, "fsdp"),
        P("dp", "fsdp", None),
        P("dp", "fsdp"),
        P("dp"),
        P(),
        P("fsdp", "dp"),
    )
    return jax.shard_map(
        per_device, mesh=mesh, in_specs=placed, out_specs=P("dp", "fsdp"), check_vma=False
    )
```

```python
import functools
import math

import jax
import jax.numpy as jnp
from jax import lax
from jax.experimental import pallas as pl
from jax.experimental.pallas import tpu as pltpu
from jax.sharding import PartitionSpec as P

BF16, F32, I32 = jnp.bfloat16, jnp.float32, jnp.int32
NT = (((1,), (1,)), ((), ()))
NN = (((1,), (0,)), ((), ()))
MIB = 1024 * 1024
FULL_MIB = 58


def dot(a, b, dims=NN):
    return lax.dot_general(a, b, dims, preferred_element_type=F32)


def sign_bits(seed, table, row0, rows, cols):
    a = lax.broadcasted_iota(I32, (1, rows), 1) + row0
    b = lax.broadcasted_iota(I32, (cols, 1), 0)
    h = a * 1103515245 + (b * 12345 + (seed * 69069 + table * 362437))
    h = h ^ lax.shift_right_logical(h, jnp.int32(15))
    h = h * 739982445
    h = h ^ lax.shift_right_logical(h, jnp.int32(13))
    return (h & 512) != 0


def signs(seed, table, row0, rows, cols):
    return jnp.where(sign_bits(seed, table, row0, rows, cols), 1.0, -1.0)


def split(v):
    hi = v.astype(BF16)
    return hi, (v - hi.astype(F32)).astype(BF16)


def prep_kernel(me, four_at, z_at, keys, gain, down, up, out):
    shard = down.shape[0]
    rows = shard // 128
    own_gain = gain[pl.ds(pl.multiple_of(me[0] * rows, rows), rows), :]
    s3 = signs(keys[1], 3, 0, down.shape[1], 32).astype(BF16)
    wb = dot(s3, down[...], NT)
    wb = jnp.concatenate(
        [wb[:, 128 * q : 128 * q + 128] * own_gain[q : q + 1, :] for q in range(rows)],
        axis=1,
    )
    s2 = signs(keys[0], 2, 0, up.shape[0], 64).astype(BF16)
    hi, lo = split(dot(s2, up[...]))
    wg = jnp.concatenate(
        [w[16 * q : 16 * q + 16] for w in (hi, lo) for q in range(4)], axis=1
    )
    both = jnp.concatenate([wb.astype(BF16), wg], axis=0)
    for n in range(out.shape[0]):
        out[n] = both


def copies_of(pairs, sems):
    return [
        pltpu.make_async_copy(a, b, sems.at[n]) for n, (a, b) in enumerate(pairs)
    ]


def x_pieces(x, held):
    steps, _, chunk = held.shape
    return [
        (x.at[:, chunk * n : chunk * n + chunk], held.at[n]) for n in range(steps)
    ]


def early_kernel(keys, gain_in, x_in, acc, sq, x, gain, table, sems):
    steps, tokens, chunk = x.shape
    width = steps * chunk
    copies = copies_of([(gain_in, gain)] + x_pieces(x_in, x), sems)
    for copy in copies:
        copy.start()
    copies[0].wait()
    for n in range(0, width, 128):
        gain_row = gain[n // 128 : n // 128 + 1, :]
        gain_hi = gain_row.astype(BF16).astype(F32)
        gain_lo = gain_row - gain_hi
        plus = sign_bits(keys[0], 1, n, 128, 64)
        table[0:64, n : n + 128] = jnp.where(plus, gain_hi, -gain_hi).astype(BF16)
        table[64:128, n : n + 128] = jnp.where(plus, gain_lo, -gain_lo).astype(BF16)
    acc[...] = jnp.zeros_like(acc)
    sq[...] = jnp.zeros_like(sq)
    @pl.loop(0, steps // 2)
    def _(pair):
        both = [2 * pair, 2 * pair + 1]
        columns = [pl.ds(pl.multiple_of(n * chunk, chunk), chunk) for n in both]
        for n, c in zip(both, columns):
            pltpu.make_async_copy(x_in.at[:, c], x.at[n], sems.at[1 + n]).wait()
        acc[...] += dot(x[both[0]], table[:, columns[0]], NT) + dot(
            x[both[1]], table[:, columns[1]], NT
        )
        for t in range(0, tokens, 64):
            total = sq[t : t + 64, :]
            for n in both:
                for c in range(0, chunk, 128):
                    piece = x[n, t : t + 64, c : c + 128].astype(F32)
                    total = total + piece * piece
            sq[t : t + 64, :] = total


def main_kernel(
    me, keys, lengths, index_in, acc_in, sq_in, w_in, g_in, x_in, out_hbm,
    index, acc, sq, w, g, x, out, xt, ua, ub, sems, out_sems,
):
    steps, tokens, chunk = x.shape
    width, gwidth = steps * chunk, g.shape[1]
    half = tokens // 2
    copies = copies_of(
        [(index_in, index), (acc_in, acc), (sq_in, sq), (w_in, w), (g_in, g)]
        + x_pieces(x_in, x),
        sems,
    )
    for copy in copies:
        copy.start()

    s4 = signs(keys[1], 4, 0, gwidth, 128).astype(BF16)
    position = me[0] * half + lax.broadcasted_iota(I32, (8, half), 1)
    example = lax.broadcasted_iota(I32, (8, half), 0)
    copies[0].wait()
    m0, m1 = (
        jnp.where(
            (index[n : n + 1, :] == example) & (position < lengths[n]), 1.0, 0.0
        )
        for n in range(2)
    )
    zero = jnp.zeros((8, half), F32)
    m8 = jnp.concatenate([m0, m1], axis=1)
    m16 = jnp.concatenate(
        [jnp.concatenate([m0, zero], axis=1), jnp.concatenate([zero, m1], axis=1)],
        axis=0,
    )
    copies[1].wait()
    copies[2].wait()
    mean_sq = jnp.sum(sq[...].T, axis=0, keepdims=True) * (1.0 / width)
    r = lax.rsqrt(mean_sq + 1e-05)
    first = acc[...].T
    xs = (first[0:64] + first[64:128]) * (r * (1.0 / math.sqrt(width)))
    hi = xs.astype(BF16).astype(F32)
    xt[0, 0:64] = hi
    xt[1, 0:64] = xs - hi
    for p in range(2):
        for i in range(32):
            ua[p, 16 * i : 16 * i + 16, :] = jnp.concatenate(
                [
                    xt[p, 2 * i : 2 * i + 1, :] * m8,
                    xt[p, 2 * i + 1 : 2 * i + 2, :] * m8,
                ],
                axis=0,
            ).astype(BF16)

    copies[3].wait()
    w_g = jnp.concatenate(
        [
            jnp.concatenate(
                [w[n, 32:48, 128 * q : 128 * q + 128] for q in range(8)], axis=0
            )
            for n in range(steps)
        ],
        axis=1,
    )
    copies[4].wait()
    pg = dot(g[...], jnp.concatenate([w_g, s4], axis=0), NT)
    two = pg[:, 0:128] * (1.0 / math.sqrt(128))
    two = two + pltpu.roll(two, 64, 1)
    row = lax.broadcasted_iota(I32, (tokens, 128), 0) >= half
    lane = lax.broadcasted_iota(I32, (tokens, 128), 1) >= 64
    va = jnp.concatenate(split(jnp.where(row == lane, two, 0.0)), axis=1)
    fa = dot(ua[0], va)
    fa = fa[:, 0:128] + fa[:, 128:256] + dot(ua[1], va[:, 0:128])
    for n in range(8):
        out[n, 0:64, :] = fa[64 * n : 64 * n + 64]
    done = [
        pltpu.make_async_copy(
            out.at[:, 64 * n : 64 * n + 64], out_hbm.at[:, 64 * n : 64 * n + 64], out_sems.at[n]
        )
        for n in range(2)
    ]
    done[0].start()
    vb = jnp.concatenate(split(pg[:, 128:256] * (1.0 / math.sqrt(gwidth))), axis=1)

    total = None
    for n in range(steps):
        copies[5 + n].wait()
        p = dot(w[n, 0:32, :], x[n], NT)
        total = p if total is None else total + p
    hs = total * (r * (1.0 / math.sqrt(128)))
    hi = hs.astype(BF16).astype(F32)
    xt[0, 64:96] = hi
    xt[1, 64:96] = hs - hi
    for p in range(2):
        for i in range(32):
            ub[p, 16 * i : 16 * i + 16, :] = (
                xt[p, 64 + i : 65 + i, :] * m16
            ).astype(BF16)
    fb = dot(ub[0], vb)
    fb = fb[:, 0:128] + fb[:, 128:256] + dot(ub[1], vb[:, 0:128])
    for n in range(8):
        out[n, 64:128, :] = fb[64 * n : 64 * n + 64]
    done[1].start()
    for copy in done:
        copy.wait()


def sum_kernel(me, parts, own, one, two, three, held):
    total = parts[0]
    for n in range(1, parts.shape[0]):
        total = total + parts[n]
    low = lax.broadcasted_iota(I32, (8, 128), 1) < 64
    for c in range(2):
        lanes = [[], []]
        for i in range(2):
            at = 32 * c + 16 * i
            u, v = total[at : at + 8], total[at + 8 : at + 16]
            lanes[0].append(jnp.where(low, u, pltpu.roll(v, 64, 1)))
            lanes[1].append(jnp.where(low, pltpu.roll(u, 64, 1), v))
        held[c] = jnp.concatenate(
            [jnp.concatenate(p, axis=1) for p in lanes], axis=0
        ).astype(BF16)
        at = 64 + 32 * c
        held[2 + c] = jnp.concatenate(
            [total[at : at + 16], total[at + 16 : at + 32]], axis=1
        ).astype(BF16)
    for k, ref in enumerate((own, one, two, three)):
        ref[...] = held[me[0] ^ k]


def score_kernel(at, feats, *rest):
    refs, (own, one, two, three) = rest[:-4], rest[-4:]
    dots = esq = rsq = None
    for k, ref in enumerate(refs):
        f, b = feats[(at[0] + 8 - k) & 7], ref[...]
        fw, bw = f.astype(F32), b.astype(F32)
        d = dot(f, b, NT)
        e2 = fw * fw
        e2 = e2[:, 0:128] + e2[:, 128:256]
        b2 = bw * bw
        b2 = b2[:, 0:128] + b2[:, 128:256]
        dots = d if dots is None else dots + d
        esq = e2 if esq is None else esq + e2
        rsq = b2 if rsq is None else rsq + b2
    esq = jnp.broadcast_to(jnp.sum(esq, axis=1, keepdims=True), (64, 128))
    rsq = jnp.sum(rsq.T, axis=0, keepdims=True)
    rows = jnp.concatenate(
        [rsq[:, 128 * q : 128 * q + 128] for q in range(4)]
        + [jnp.zeros((12, 128), F32)],
        axis=0,
    )
    for k, ref in enumerate((own, one, two, three)):
        ref[:, 0:512] = dots[16 * k : 16 * k + 16]
        ref[:, 512:640] = esq[16 * k : 16 * k + 16]
        ref[:, 640:768] = rows


def final_kernel(own, one, two, three, out):
    total = (own[...] + one[...]) + (two[...] + three[...])
    enorm = lax.rsqrt(total[:, 512:640] + 1e-06)
    rnorm = lax.rsqrt(total[:, 640:768] + 1e-06)
    for q in range(4):
        out[:, 128 * q : 128 * q + 128] = (
            total[:, 128 * q : 128 * q + 128] * enorm * rnorm[q : q + 1, :]
        )


VMEM = pl.BlockSpec(memory_space=pltpu.VMEM)
SMEM = pl.BlockSpec(memory_space=pltpu.SMEM)
HBM = pl.BlockSpec(memory_space=pltpu.HBM)


def shape(dims, kind):
    return jax.ShapeDtypeStruct(dims, kind)


def kernel(body, name, out, ins, scratch=(), vmem=4, flops=0, nbytes=0, outs=VMEM):
    single = not isinstance(out, list)
    return pl.pallas_call(
        body,
        out_shape=out,
        in_specs=ins,
        out_specs=outs if single else [outs] * len(out),
        scratch_shapes=scratch,
        compiler_params=pltpu.CompilerParams(vmem_limit_bytes=vmem * MIB),
        cost_estimate=pl.CostEstimate(flops=flops, bytes_accessed=nbytes, transcendentals=0),
        name=name,
    )


def per_device(
    residual,
    input_norm_gain,
    adapter_entry_matrix,
    adapter_exit_matrix,
    value_output_gradient,
    position_example_index,
    live_row_length,
    random_sketch_keys,
    reference_gradients,
):
    seq_count, local_len, width = residual.shape
    tokens = seq_count * local_len
    value_width = value_output_gradient.shape[2]
    n_fsdp, n_dp = lax.axis_size("fsdp"), lax.axis_size("dp")
    fsdp, dp = lax.axis_index("fsdp"), lax.axis_index("dp")
    top = n_dp // 2
    fsdp_at = fsdp.reshape(1)
    z_at = (dp // 2 % (top // 2)).reshape(1)
    four_at = (dp // top * 2 + dp % 2).reshape(1)
    swaps = [[(n, n ^ flip) for n in range(n_dp)] for flip in (1, top, top + 1)]
    up, down = (
        [(n, n // top * top + (n + 2 * way) % top) for n in range(n_dp)] for way in (1, -1)
    )
    tie = lax.optimization_barrier

    x = residual.reshape(tokens, width)
    g = value_output_gradient.reshape(tokens, value_width)
    gain = input_norm_gain.reshape(width // 128, 128)
    chunk = width // n_fsdp

    refs_up = [lax.ppermute(reference_gradients, "dp", up)]
    refs_down = [lax.ppermute(reference_gradients, "dp", down)]

    weights = kernel(
        prep_kernel,
        "prep",
        shape((n_fsdp, 48, chunk), BF16),
        [SMEM] * 4 + [VMEM] * 3,
        vmem=FULL_MIB,
    )(fsdp_at, four_at, z_at, random_sketch_keys, gain, adapter_entry_matrix, adapter_exit_matrix)
    weights = lax.all_to_all(weights, "fsdp", 0, 0)

    early = kernel(
        early_kernel,
        "early",
        [shape((tokens, 128), F32)] * 2,
        [SMEM] + [HBM] * 2,
        [
            pltpu.VMEM((n_fsdp, tokens, chunk), BF16),
            pltpu.VMEM((width // 128, 128), F32),
            pltpu.VMEM((128, width), BF16),
            pltpu.SemaphoreType.DMA((1 + n_fsdp,)),
        ],
        vmem=FULL_MIB,
        flops=2 * tokens * width * 256,
        nbytes=12 * MIB,
    )(random_sketch_keys, gain, x)
    early, refs_up[0], refs_down[0] = tie((early, refs_up[0], refs_down[0]))
    refs_up.append(lax.ppermute(refs_up[0], "dp", up))
    refs_down.append(lax.ppermute(refs_down[0], "dp", down))

    features = kernel(
        main_kernel,
        "features",
        shape((8, 128, 128), F32),
        [SMEM] * 3 + [HBM] * 6,
        [
            pltpu.VMEM((seq_count, local_len), I32),
            pltpu.VMEM((tokens, 128), F32),
            pltpu.VMEM((tokens, 128), F32),
            pltpu.VMEM((n_fsdp, 48, chunk), BF16),
            pltpu.VMEM((tokens, value_width), BF16),
            pltpu.VMEM((n_fsdp, tokens, chunk), BF16),
            pltpu.VMEM((8, 128, 128), F32),
            pltpu.VMEM((2, 96, tokens), F32),
            pltpu.VMEM((2, 512, tokens), BF16),
            pltpu.VMEM((2, 512, tokens), BF16),
            pltpu.SemaphoreType.DMA((5 + n_fsdp,)),
            pltpu.SemaphoreType.DMA((2,)),
        ],
        vmem=FULL_MIB,
        flops=2 * tokens * width * 256,
        nbytes=12 * MIB,
        outs=HBM,
    )(
        fsdp_at,
        random_sketch_keys,
        live_row_length,
        position_example_index,
        *early,
        weights,
        g,
        x,
    )
    features, refs_up[1], refs_down[1] = tie((features, refs_up[1], refs_down[1]))
    refs_up.append(lax.ppermute(refs_up[1], "dp", up))
    refs_down.append(lax.ppermute(refs_down[1], "dp", down))
    features = lax.all_to_all(features, "fsdp", 0, 0)

    pieces = kernel(
        sum_kernel,
        "sum_features",
        [shape((16, 256), BF16)] * 4,
        [SMEM, VMEM],
        [pltpu.VMEM((4, 16, 256), BF16)],
    )(four_at, features)
    pieces = [pieces[0]] + [
        lax.ppermute(piece, "dp", swap) for piece, swap in zip(pieces[1:], swaps)
    ]
    feats = jnp.concatenate(pieces, axis=0)
    feats, refs_up[2], refs_down[2] = tie((feats, refs_up[2], refs_down[2]))
    refs_up.append(lax.ppermute(refs_up[2], "dp", up))
    feats = jnp.broadcast_to(feats[None], (n_fsdp,) + feats.shape)
    feats = lax.all_to_all(feats, "fsdp", 0, 0)

    refs = [reference_gradients] + refs_up + refs_down[::-1]
    pieces = kernel(
        score_kernel,
        "partial_scores",
        [shape((16, 768), F32)] * 4,
        [SMEM] + [VMEM] * 9,
        vmem=8,
    )(z_at, feats, *refs)
    pieces = [pieces[0]] + [
        lax.ppermute(piece, "dp", swap) for piece, swap in zip(pieces[1:], swaps)
    ]
    return kernel(
        final_kernel,
        "scores",
        shape((16, reference_gradients.shape[0]), F32),
        [VMEM] * 4,
    )(*pieces)


def solution(mesh):
    placed = (
        P("dp", "fsdp", None),
        P(),
        P("fsdp", None),
        P(None, "fsdp"),
        P("dp", "fsdp", None),
        P("dp", "fsdp"),
        P("dp"),
        P(),
        P("fsdp", "dp"),
    )
    return jax.shard_map(
        per_device, mesh=mesh, in_specs=placed, out_specs=P("dp", "fsdp"), check_vma=False
    )
```

```python
import functools
import math

import jax
import jax.numpy as jnp
from jax import lax
from jax.experimental import pallas as pl
from jax.experimental.pallas import tpu as pltpu
from jax.sharding import PartitionSpec as P

BF16, F32, I32 = jnp.bfloat16, jnp.float32, jnp.int32
NT = (((1,), (1,)), ((), ()))
NN = (((1,), (0,)), ((), ()))
MIB = 1024 * 1024
FULL_MIB = 58


def dot(a, b, dims=NN):
    return lax.dot_general(a, b, dims, preferred_element_type=F32)


def sign_bits(seed, table, row0, rows, cols):
    a = lax.broadcasted_iota(I32, (1, rows), 1) + row0
    b = lax.broadcasted_iota(I32, (cols, 1), 0)
    h = a * 1103515245 + (b * 12345 + (seed * 69069 + table * 362437))
    h = h ^ lax.shift_right_logical(h, jnp.int32(15))
    h = h * 739982445
    h = h ^ lax.shift_right_logical(h, jnp.int32(13))
    return (h & 512) != 0


def signs(seed, table, row0, rows, cols):
    return jnp.where(sign_bits(seed, table, row0, rows, cols), 1.0, -1.0)


def split(v):
    hi = v.astype(BF16)
    return hi, (v - hi.astype(F32)).astype(BF16)


def prep_kernel(me, four_at, z_at, keys, gain, down, up, out):
    shard = down.shape[0]
    rows = shard // 128
    own_gain = gain[pl.ds(pl.multiple_of(me[0] * rows, rows), rows), :]
    s3 = signs(keys[1], 3, 0, down.shape[1], 32).astype(BF16)
    wb = dot(s3, down[...], NT)
    wb = jnp.concatenate(
        [wb[:, 128 * q : 128 * q + 128] * own_gain[q : q + 1, :] for q in range(rows)],
        axis=1,
    )
    s2 = signs(keys[0], 2, 0, up.shape[0], 64).astype(BF16)
    hi, lo = split(dot(s2, up[...]))
    wg = jnp.concatenate(
        [w[16 * q : 16 * q + 16] for w in (hi, lo) for q in range(4)], axis=1
    )
    both = jnp.concatenate([wb.astype(BF16), wg], axis=0)
    for n in range(out.shape[0]):
        out[n] = both


def copies_of(pairs, sems):
    return [
        pltpu.make_async_copy(a, b, sems.at[n]) for n, (a, b) in enumerate(pairs)
    ]


def x_pieces(x, held):
    steps, _, chunk = held.shape
    return [
        (x.at[:, chunk * n : chunk * n + chunk], held.at[n]) for n in range(steps)
    ]


def early_kernel(keys, gain_in, x_in, acc, sq, x, gain, table, sems):
    steps, tokens, chunk = x.shape
    width = steps * chunk
    copies = copies_of([(gain_in, gain)] + x_pieces(x_in, x), sems)
    for copy in copies:
        copy.start()
    copies[0].wait()
    for n in range(0, width, 128):
        gain_row = gain[n // 128 : n // 128 + 1, :]
        gain_hi = gain_row.astype(BF16).astype(F32)
        gain_lo = gain_row - gain_hi
        plus = sign_bits(keys[0], 1, n, 128, 64)
        table[0:64, n : n + 128] = jnp.where(plus, gain_hi, -gain_hi).astype(BF16)
        table[64:128, n : n + 128] = jnp.where(plus, gain_lo, -gain_lo).astype(BF16)
    acc[...] = jnp.zeros_like(acc)
    sq[...] = jnp.zeros_like(sq)
    @pl.loop(0, steps // 2)
    def _(pair):
        both = [2 * pair, 2 * pair + 1]
        columns = [pl.ds(pl.multiple_of(n * chunk, chunk), chunk) for n in both]
        for n, c in zip(both, columns):
            pltpu.make_async_copy(x_in.at[:, c], x.at[n], sems.at[1 + n]).wait()
        acc[...] += dot(x[both[0]], table[:, columns[0]], NT) + dot(
            x[both[1]], table[:, columns[1]], NT
        )
        for t in range(0, tokens, 64):
            total = sq[t : t + 64, :]
            for n in both:
                for c in range(0, chunk, 128):
                    piece = x[n, t : t + 64, c : c + 128].astype(F32)
                    total = total + piece * piece
            sq[t : t + 64, :] = total


def main_kernel(
    me, keys, lengths, index_in, acc_in, sq_in, w_in, g_in, x_in, out_hbm,
    index, acc, sq, w, g, x, out, xt, ua, ub, sems, out_sems,
):
    steps, tokens, chunk = x.shape
    width, gwidth = steps * chunk, g.shape[1]
    half = tokens // 2
    copies = copies_of(
        [(index_in, index), (acc_in, acc), (sq_in, sq), (w_in, w), (g_in, g)]
        + x_pieces(x_in, x),
        sems,
    )
    for copy in copies:
        copy.start()

    s4 = signs(keys[1], 4, 0, gwidth, 128).astype(BF16)
    position = me[0] * half + lax.broadcasted_iota(I32, (8, half), 1)
    example = lax.broadcasted_iota(I32, (8, half), 0)
    copies[0].wait()
    m0, m1 = (
        jnp.where(
            (index[n : n + 1, :] == example) & (position < lengths[n]), 1.0, 0.0
        )
        for n in range(2)
    )
    zero = jnp.zeros((8, half), F32)
    m8 = jnp.concatenate([m0, m1], axis=1)
    m16 = jnp.concatenate(
        [jnp.concatenate([m0, zero], axis=1), jnp.concatenate([zero, m1], axis=1)],
        axis=0,
    )
    copies[1].wait()
    copies[2].wait()
    mean_sq = jnp.sum(sq[...].T, axis=0, keepdims=True) * (1.0 / width)
    r = lax.rsqrt(mean_sq + 1e-05)
    first = acc[...].T
    xs = (first[0:64] + first[64:128]) * (r * (1.0 / math.sqrt(width)))
    hi = xs.astype(BF16).astype(F32)
    xt[0, 0:64] = hi
    xt[1, 0:64] = xs - hi
    for p in range(2):
        for i in range(32):
            ua[p, 16 * i : 16 * i + 16, :] = jnp.concatenate(
                [
                    xt[p, 2 * i : 2 * i + 1, :] * m8,
                    xt[p, 2 * i + 1 : 2 * i + 2, :] * m8,
                ],
                axis=0,
            ).astype(BF16)

    copies[3].wait()
    w_g = jnp.concatenate(
        [
            jnp.concatenate(
                [w[n, 32:48, 128 * q : 128 * q + 128] for q in range(8)], axis=0
            )
            for n in range(steps)
        ],
        axis=1,
    )
    copies[4].wait()
    pg = dot(g[...], jnp.concatenate([w_g, s4], axis=0), NT)
    two = pg[:, 0:128] * (1.0 / math.sqrt(128))
    two = two + pltpu.roll(two, 64, 1)
    row = lax.broadcasted_iota(I32, (tokens, 128), 0) >= half
    lane = lax.broadcasted_iota(I32, (tokens, 128), 1) >= 64
    va = jnp.concatenate(split(jnp.where(row == lane, two, 0.0)), axis=1)
    fa = dot(ua[0], va)
    fa = fa[:, 0:128] + fa[:, 128:256] + dot(ua[1], va[:, 0:128])
    for n in range(8):
        out[n, 0:64, :] = fa[64 * n : 64 * n + 64]
    done = [
        pltpu.make_async_copy(
            out.at[:, 64 * n : 64 * n + 64], out_hbm.at[:, 64 * n : 64 * n + 64], out_sems.at[n]
        )
        for n in range(2)
    ]
    done[0].start()
    vb = jnp.concatenate(split(pg[:, 128:256] * (1.0 / math.sqrt(gwidth))), axis=1)

    total = None
    for n in range(steps):
        copies[5 + n].wait()
        p = dot(w[n, 0:32, :], x[n], NT)
        total = p if total is None else total + p
    hs = total * (r * (1.0 / math.sqrt(128)))
    hi = hs.astype(BF16).astype(F32)
    xt[0, 64:96] = hi
    xt[1, 64:96] = hs - hi
    for p in range(2):
        for i in range(32):
            ub[p, 16 * i : 16 * i + 16, :] = (
                xt[p, 64 + i : 65 + i, :] * m16
            ).astype(BF16)
    fb = dot(ub[0], vb)
    fb = fb[:, 0:128] + fb[:, 128:256] + dot(ub[1], vb[:, 0:128])
    for n in range(8):
        out[n, 64:128, :] = fb[64 * n : 64 * n + 64]
    done[1].start()
    for copy in done:
        copy.wait()


def sum_kernel(me, parts, own, one, two, three, held):
    total = parts[0]
    for n in range(1, parts.shape[0]):
        total = total + parts[n]
    low = lax.broadcasted_iota(I32, (8, 128), 1) < 64
    for c in range(2):
        lanes = [[], []]
        for i in range(2):
            at = 32 * c + 16 * i
            u, v = total[at : at + 8], total[at + 8 : at + 16]
            lanes[0].append(jnp.where(low, u, pltpu.roll(v, 64, 1)))
            lanes[1].append(jnp.where(low, pltpu.roll(u, 64, 1), v))
        held[c] = jnp.concatenate(
            [jnp.concatenate(p, axis=1) for p in lanes], axis=0
        ).astype(BF16)
        at = 64 + 32 * c
        held[2 + c] = jnp.concatenate(
            [total[at : at + 16], total[at + 16 : at + 32]], axis=1
        ).astype(BF16)
    for k, ref in enumerate((own, one, two, three)):
        ref[...] = held[me[0] ^ k]


def score_kernel(at, feats, *rest):
    refs, (own, one, two, three) = rest[:-4], rest[-4:]
    dots = esq = rsq = None
    for k, ref in enumerate(refs):
        f, b = feats[(at[0] + 8 - k) & 7], ref[...]
        fw, bw = f.astype(F32), b.astype(F32)
        d = dot(f, b, NT)
        e2 = fw * fw
        e2 = e2[:, 0:128] + e2[:, 128:256]
        b2 = bw * bw
        b2 = b2[:, 0:128] + b2[:, 128:256]
        dots = d if dots is None else dots + d
        esq = e2 if esq is None else esq + e2
        rsq = b2 if rsq is None else rsq + b2
    esq = jnp.broadcast_to(jnp.sum(esq, axis=1, keepdims=True), (64, 128))
    rsq = jnp.sum(rsq.T, axis=0, keepdims=True)
    rows = jnp.concatenate(
        [rsq[:, 128 * q : 128 * q + 128] for q in range(4)]
        + [jnp.zeros((12, 128), F32)],
        axis=0,
    )
    for k, ref in enumerate((own, one, two, three)):
        ref[:, 0:512] = dots[16 * k : 16 * k + 16]
        ref[:, 512:640] = esq[16 * k : 16 * k + 16]
        ref[:, 640:768] = rows


def final_kernel(own, one, two, three, out):
    total = (own[...] + one[...]) + (two[...] + three[...])
    enorm = lax.rsqrt(total[:, 512:640] + 1e-06)
    rnorm = lax.rsqrt(total[:, 640:768] + 1e-06)
    for q in range(4):
        out[:, 128 * q : 128 * q + 128] = (
            total[:, 128 * q : 128 * q + 128] * enorm * rnorm[q : q + 1, :]
        )


VMEM = pl.BlockSpec(memory_space=pltpu.VMEM)
SMEM = pl.BlockSpec(memory_space=pltpu.SMEM)
HBM = pl.BlockSpec(memory_space=pltpu.HBM)


def shape(dims, kind):
    return jax.ShapeDtypeStruct(dims, kind)


def kernel(body, name, out, ins, scratch=(), vmem=4, flops=0, nbytes=0, outs=VMEM):
    single = not isinstance(out, list)
    return pl.pallas_call(
        body,
        out_shape=out,
        in_specs=ins,
        out_specs=outs if single else [outs] * len(out),
        scratch_shapes=scratch,
        compiler_params=pltpu.CompilerParams(vmem_limit_bytes=vmem * MIB),
        cost_estimate=pl.CostEstimate(flops=flops, bytes_accessed=nbytes, transcendentals=0),
        name=name,
    )


def per_device(
    residual,
    input_norm_gain,
    adapter_entry_matrix,
    adapter_exit_matrix,
    value_output_gradient,
    position_example_index,
    live_row_length,
    random_sketch_keys,
    reference_gradients,
):
    seq_count, local_len, width = residual.shape
    tokens = seq_count * local_len
    value_width = value_output_gradient.shape[2]
    n_fsdp, n_dp = lax.axis_size("fsdp"), lax.axis_size("dp")
    fsdp, dp = lax.axis_index("fsdp"), lax.axis_index("dp")
    top = n_dp // 2
    fsdp_at = fsdp.reshape(1)
    z_at = (dp // 2 % (top // 2)).reshape(1)
    four_at = (dp // top * 2 + dp % 2).reshape(1)
    swaps = [[(n, n ^ flip) for n in range(n_dp)] for flip in (1, top, top + 1)]
    up, down = (
        [(n, n // top * top + (n + 2 * way) % top) for n in range(n_dp)] for way in (1, -1)
    )

    x = residual.reshape(tokens, width)
    g = value_output_gradient.reshape(tokens, value_width)
    gain = input_norm_gain.reshape(width // 128, 128)
    chunk = width // n_fsdp

    refs_up = [lax.ppermute(reference_gradients, "dp", up)]
    refs_down = [lax.ppermute(reference_gradients, "dp", down)]

    weights = kernel(
        prep_kernel,
        "prep",
        shape((n_fsdp, 48, chunk), BF16),
        [SMEM] * 4 + [VMEM] * 3,
        vmem=FULL_MIB,
    )(fsdp_at, four_at, z_at, random_sketch_keys, gain, adapter_entry_matrix, adapter_exit_matrix)
    weights = lax.all_to_all(weights, "fsdp", 0, 0)

    early = kernel(
        early_kernel,
        "early",
        [shape((tokens, 128), F32)] * 2,
        [SMEM] + [HBM] * 2,
        [
            pltpu.VMEM((n_fsdp, tokens, chunk), BF16),
            pltpu.VMEM((width // 128, 128), F32),
            pltpu.VMEM((128, width), BF16),
            pltpu.SemaphoreType.DMA((1 + n_fsdp,)),
        ],
        vmem=FULL_MIB,
        flops=2 * tokens * width * 256,
        nbytes=12 * MIB,
    )(random_sketch_keys, gain, x)
    refs_up.append(lax.ppermute(refs_up[0], "dp", up))
    refs_down.append(lax.ppermute(refs_down[0], "dp", down))

    features = kernel(
        main_kernel,
        "features",
        shape((8, 128, 128), F32),
        [SMEM] * 3 + [HBM] * 6,
        [
            pltpu.VMEM((seq_count, local_len), I32),
            pltpu.VMEM((tokens, 128), F32),
            pltpu.VMEM((tokens, 128), F32),
            pltpu.VMEM((n_fsdp, 48, chunk), BF16),
            pltpu.VMEM((tokens, value_width), BF16),
            pltpu.VMEM((n_fsdp, tokens, chunk), BF16),
            pltpu.VMEM((8, 128, 128), F32),
            pltpu.VMEM((2, 96, tokens), F32),
            pltpu.VMEM((2, 512, tokens), BF16),
            pltpu.VMEM((2, 512, tokens), BF16),
            pltpu.SemaphoreType.DMA((5 + n_fsdp,)),
            pltpu.SemaphoreType.DMA((2,)),
        ],
        vmem=FULL_MIB,
        flops=2 * tokens * width * 256,
        nbytes=12 * MIB,
        outs=HBM,
    )(
        fsdp_at,
        random_sketch_keys,
        live_row_length,
        position_example_index,
        *early,
        weights,
        g,
        x,
    )
    refs_up.append(lax.ppermute(refs_up[1], "dp", up))
    refs_down.append(lax.ppermute(refs_down[1], "dp", down))
    features = lax.all_to_all(features, "fsdp", 0, 0)

    pieces = kernel(
        sum_kernel,
        "sum_features",
        [shape((16, 256), BF16)] * 4,
        [SMEM, VMEM],
        [pltpu.VMEM((4, 16, 256), BF16)],
    )(four_at, features)
    pieces = [pieces[0]] + [
        lax.ppermute(piece, "dp", swap) for piece, swap in zip(pieces[1:], swaps)
    ]
    feats = jnp.concatenate(pieces, axis=0)
    refs_up.append(lax.ppermute(refs_up[2], "dp", up))
    feats = jnp.broadcast_to(feats[None], (n_fsdp,) + feats.shape)
    feats = lax.all_to_all(feats, "fsdp", 0, 0)

    refs = [reference_gradients] + refs_up + refs_down[::-1]
    pieces = kernel(
        score_kernel,
        "partial_scores",
        [shape((16, 768), F32)] * 4,
        [SMEM] + [VMEM] * 9,
        vmem=8,
    )(z_at, feats, *refs)
    pieces = [pieces[0]] + [
        lax.ppermute(piece, "dp", swap) for piece, swap in zip(pieces[1:], swaps)
    ]
    return kernel(
        final_kernel,
        "scores",
        shape((16, reference_gradients.shape[0]), F32),
        [VMEM] * 4,
    )(*pieces)


def solution(mesh):
    placed = (
        P("dp", "fsdp", None),
        P(),
        P("fsdp", None),
        P(None, "fsdp"),
        P("dp", "fsdp", None),
        P("dp", "fsdp"),
        P("dp"),
        P(),
        P("fsdp", "dp"),
    )
    return jax.shard_map(
        per_device, mesh=mesh, in_specs=placed, out_specs=P("dp", "fsdp"), check_vma=False
    )
```

```python
import functools
import math

import jax
import jax.numpy as jnp
from jax import lax
from jax.experimental import pallas as pl
from jax.experimental.pallas import tpu as pltpu
from jax.sharding import PartitionSpec as P

BF16, F32, I32 = jnp.bfloat16, jnp.float32, jnp.int32
NT = (((1,), (1,)), ((), ()))
NN = (((1,), (0,)), ((), ()))
MIB = 1024 * 1024
FULL_MIB = 58


def dot(a, b, dims=NN):
    return lax.dot_general(a, b, dims, preferred_element_type=F32)


def sign_bits(seed, table, row0, rows, cols):
    a = lax.broadcasted_iota(I32, (1, rows), 1) + row0
    b = lax.broadcasted_iota(I32, (cols, 1), 0)
    h = a * 1103515245 + (b * 12345 + (seed * 69069 + table * 362437))
    h = h ^ lax.shift_right_logical(h, jnp.int32(15))
    h = h * 739982445
    h = h ^ lax.shift_right_logical(h, jnp.int32(13))
    return (h & 512) != 0


def signs(seed, table, row0, rows, cols):
    return jnp.where(sign_bits(seed, table, row0, rows, cols), 1.0, -1.0)


def split(v):
    hi = v.astype(BF16)
    return hi, (v - hi.astype(F32)).astype(BF16)


def prep_kernel(me, four_at, z_at, keys, gain, down, up, out):
    shard = down.shape[0]
    rows = shard // 128
    own_gain = gain[pl.ds(pl.multiple_of(me[0] * rows, rows), rows), :]
    s3 = signs(keys[1], 3, 0, down.shape[1], 32).astype(BF16)
    wb = dot(s3, down[...], NT)
    wb = jnp.concatenate(
        [wb[:, 128 * q : 128 * q + 128] * own_gain[q : q + 1, :] for q in range(rows)],
        axis=1,
    )
    s2 = signs(keys[0], 2, 0, up.shape[0], 64).astype(BF16)
    hi, lo = split(dot(s2, up[...]))
    wg = jnp.concatenate(
        [w[16 * q : 16 * q + 16] for w in (hi, lo) for q in range(4)], axis=1
    )
    both = jnp.concatenate([wb.astype(BF16), wg], axis=0)
    for n in range(out.shape[0]):
        out[n] = both


def copies_of(pairs, sems):
    return [
        pltpu.make_async_copy(a, b, sems.at[n]) for n, (a, b) in enumerate(pairs)
    ]


def x_pieces(x, held):
    steps, _, chunk = held.shape
    return [
        (x.at[:, chunk * n : chunk * n + chunk], held.at[n]) for n in range(steps)
    ]


def early_kernel(keys, gain_in, x_in, acc, sq, x, gain, table, sems):
    steps, tokens, chunk = x.shape
    width = steps * chunk
    copies = copies_of([(gain_in, gain)] + x_pieces(x_in, x), sems)
    for copy in copies:
        copy.start()
    for n in range(0, width, 128):
        table[0:64, n : n + 128] = signs(keys[0], 1, n, 128, 64).astype(BF16)
    copies[0].wait()
    for n in range(0, width, 128):
        gain_row = gain[n // 128 : n // 128 + 1, :]
        gain_hi = gain_row.astype(BF16)
        gain_lo = (gain_row - gain_hi.astype(F32)).astype(BF16)
        plus = table[0:64, n : n + 128]
        table[64:128, n : n + 128] = plus * gain_lo
        table[0:64, n : n + 128] = plus * gain_hi
    acc[...] = jnp.zeros_like(acc)
    sq[...] = jnp.zeros_like(sq)
    @pl.loop(0, steps // 2)
    def _(pair):
        both = [2 * pair, 2 * pair + 1]
        columns = [pl.ds(pl.multiple_of(n * chunk, chunk), chunk) for n in both]
        for n, c in zip(both, columns):
            pltpu.make_async_copy(x_in.at[:, c], x.at[n], sems.at[1 + n]).wait()
        acc[...] += dot(x[both[0]], table[:, columns[0]], NT) + dot(
            x[both[1]], table[:, columns[1]], NT
        )
        for t in range(0, tokens, 64):
            total = sq[t : t + 64, :]
            for n in both:
                for c in range(0, chunk, 128):
                    piece = x[n, t : t + 64, c : c + 128].astype(F32)
                    total = total + piece * piece
            sq[t : t + 64, :] = total


def main_kernel(
    me, keys, lengths, index_in, acc_in, sq_in, w_in, g_in, x_in, out_hbm,
    index, acc, sq, w, g, x, out, xt, ua, ub, sems, out_sems,
):
    steps, tokens, chunk = x.shape
    width, gwidth = steps * chunk, g.shape[1]
    half = tokens // 2
    copies = copies_of(
        [(index_in, index), (acc_in, acc), (sq_in, sq), (w_in, w), (g_in, g)]
        + x_pieces(x_in, x),
        sems,
    )
    for copy in copies:
        copy.start()

    s4 = signs(keys[1], 4, 0, gwidth, 128).astype(BF16)
    position = me[0] * half + lax.broadcasted_iota(I32, (8, half), 1)
    example = lax.broadcasted_iota(I32, (8, half), 0)
    copies[0].wait()
    m0, m1 = (
        jnp.where(
            (index[n : n + 1, :] == example) & (position < lengths[n]), 1.0, 0.0
        )
        for n in range(2)
    )
    zero = jnp.zeros((8, half), F32)
    m8 = jnp.concatenate([m0, m1], axis=1)
    m16 = jnp.concatenate(
        [jnp.concatenate([m0, zero], axis=1), jnp.concatenate([zero, m1], axis=1)],
        axis=0,
    )
    copies[1].wait()
    copies[2].wait()
    mean_sq = jnp.sum(sq[...].T, axis=0, keepdims=True) * (1.0 / width)
    r = lax.rsqrt(mean_sq + 1e-05)
    first = acc[...].T
    xs = (first[0:64] + first[64:128]) * (r * (1.0 / math.sqrt(width)))
    hi = xs.astype(BF16).astype(F32)
    xt[0, 0:64] = hi
    xt[1, 0:64] = xs - hi
    for p in range(2):
        for i in range(32):
            ua[p, 16 * i : 16 * i + 16, :] = jnp.concatenate(
                [
                    xt[p, 2 * i : 2 * i + 1, :] * m8,
                    xt[p, 2 * i + 1 : 2 * i + 2, :] * m8,
                ],
                axis=0,
            ).astype(BF16)

    copies[3].wait()
    w_g = jnp.concatenate(
        [
            jnp.concatenate(
                [w[n, 32:48, 128 * q : 128 * q + 128] for q in range(8)], axis=0
            )
            for n in range(steps)
        ],
        axis=1,
    )
    copies[4].wait()
    pg = dot(g[...], jnp.concatenate([w_g, s4], axis=0), NT)
    two = pg[:, 0:128] * (1.0 / math.sqrt(128))
    two = two + pltpu.roll(two, 64, 1)
    row = lax.broadcasted_iota(I32, (tokens, 128), 0) >= half
    lane = lax.broadcasted_iota(I32, (tokens, 128), 1) >= 64
    va = jnp.concatenate(split(jnp.where(row == lane, two, 0.0)), axis=1)
    fa = dot(ua[0], va)
    fa = fa[:, 0:128] + fa[:, 128:256] + dot(ua[1], va[:, 0:128])
    for n in range(8):
        out[n, 0:64, :] = fa[64 * n : 64 * n + 64]
    done = [
        pltpu.make_async_copy(
            out.at[:, 64 * n : 64 * n + 64], out_hbm.at[:, 64 * n : 64 * n + 64], out_sems.at[n]
        )
        for n in range(2)
    ]
    done[0].start()
    vb = jnp.concatenate(split(pg[:, 128:256] * (1.0 / math.sqrt(gwidth))), axis=1)

    total = None
    for n in range(steps):
        copies[5 + n].wait()
        p = dot(w[n, 0:32, :], x[n], NT)
        total = p if total is None else total + p
    hs = total * (r * (1.0 / math.sqrt(128)))
    hi = hs.astype(BF16).astype(F32)
    xt[0, 64:96] = hi
    xt[1, 64:96] = hs - hi
    for p in range(2):
        for i in range(32):
            ub[p, 16 * i : 16 * i + 16, :] = (
                xt[p, 64 + i : 65 + i, :] * m16
            ).astype(BF16)
    fb = dot(ub[0], vb)
    fb = fb[:, 0:128] + fb[:, 128:256] + dot(ub[1], vb[:, 0:128])
    for n in range(8):
        out[n, 64:128, :] = fb[64 * n : 64 * n + 64]
    done[1].start()
    for copy in done:
        copy.wait()


def sum_kernel(me, parts, own, one, two, three, held):
    total = parts[0]
    for n in range(1, parts.shape[0]):
        total = total + parts[n]
    low = lax.broadcasted_iota(I32, (8, 128), 1) < 64
    for c in range(2):
        lanes = [[], []]
        for i in range(2):
            at = 32 * c + 16 * i
            u, v = total[at : at + 8], total[at + 8 : at + 16]
            lanes[0].append(jnp.where(low, u, pltpu.roll(v, 64, 1)))
            lanes[1].append(jnp.where(low, pltpu.roll(u, 64, 1), v))
        held[c] = jnp.concatenate(
            [jnp.concatenate(p, axis=1) for p in lanes], axis=0
        ).astype(BF16)
        at = 64 + 32 * c
        held[2 + c] = jnp.concatenate(
            [total[at : at + 16], total[at + 16 : at + 32]], axis=1
        ).astype(BF16)
    for k, ref in enumerate((own, one, two, three)):
        ref[...] = held[me[0] ^ k]


def score_kernel(at, feats, *rest):
    refs, (own, one, two, three) = rest[:-4], rest[-4:]
    dots = esq = rsq = None
    for k, ref in enumerate(refs):
        f, b = feats[(at[0] + 8 - k) & 7], ref[...]
        fw, bw = f.astype(F32), b.astype(F32)
        d = dot(f, b, NT)
        e2 = fw * fw
        e2 = e2[:, 0:128] + e2[:, 128:256]
        b2 = bw * bw
        b2 = b2[:, 0:128] + b2[:, 128:256]
        dots = d if dots is None else dots + d
        esq = e2 if esq is None else esq + e2
        rsq = b2 if rsq is None else rsq + b2
    esq = jnp.broadcast_to(jnp.sum(esq, axis=1, keepdims=True), (64, 128))
    rsq = jnp.sum(rsq.T, axis=0, keepdims=True)
    rows = jnp.concatenate(
        [rsq[:, 128 * q : 128 * q + 128] for q in range(4)]
        + [jnp.zeros((12, 128), F32)],
        axis=0,
    )
    own[:, 0:512] = dots[0:16]
    own[:, 512:640] = esq[0:16]
    own[:, 640:768] = rows
    rows_hi, rows_lo = split(rows[0:4])
    rows = jnp.concatenate(
        [rows_hi.astype(F32), rows_lo.astype(F32), rows[8:16]], axis=0
    ).astype(BF16)
    low = lax.broadcasted_iota(I32, (16, 128), 1) < 64
    for k, ref in ((1, one), (2, two), (3, three)):
        ref[:, 0:512] = dots[16 * k : 16 * k + 16].astype(BF16)
        hi, lo = split(esq[16 * k : 16 * k + 16])
        ref[:, 512:640] = jnp.where(low, hi.astype(F32), lo.astype(F32)).astype(BF16)
        ref[:, 640:768] = rows


def final_kernel(own, one, two, three, out):
    dots, esq, rsq = own[:, 0:512], own[:, 512:640], own[0:4, 640:768]
    for ref in (one, two, three):
        dots = dots + ref[:, 0:512].astype(F32)
        parts = ref[:, 512:640].astype(F32)
        esq = esq + (parts + pltpu.roll(parts, 64, 1))
        parts = ref[:, 640:768].astype(F32)
        rsq = rsq + (parts[0:4] + parts[4:8])
    enorm = lax.rsqrt(esq + 1e-06)
    rnorm = lax.rsqrt(rsq + 1e-06)
    for q in range(4):
        out[:, 128 * q : 128 * q + 128] = (
            dots[:, 128 * q : 128 * q + 128] * enorm * rnorm[q : q + 1, :]
        )


VMEM = pl.BlockSpec(memory_space=pltpu.VMEM)
SMEM = pl.BlockSpec(memory_space=pltpu.SMEM)
HBM = pl.BlockSpec(memory_space=pltpu.HBM)


def shape(dims, kind):
    return jax.ShapeDtypeStruct(dims, kind)


def kernel(body, name, out, ins, scratch=(), vmem=4, flops=0, nbytes=0, outs=VMEM):
    single = not isinstance(out, list)
    return pl.pallas_call(
        body,
        out_shape=out,
        in_specs=ins,
        out_specs=outs if single else [outs] * len(out),
        scratch_shapes=scratch,
        compiler_params=pltpu.CompilerParams(vmem_limit_bytes=vmem * MIB),
        cost_estimate=pl.CostEstimate(flops=flops, bytes_accessed=nbytes, transcendentals=0),
        name=name,
    )


def per_device(
    residual,
    input_norm_gain,
    adapter_entry_matrix,
    adapter_exit_matrix,
    value_output_gradient,
    position_example_index,
    live_row_length,
    random_sketch_keys,
    reference_gradients,
):
    seq_count, local_len, width = residual.shape
    tokens = seq_count * local_len
    value_width = value_output_gradient.shape[2]
    n_fsdp, n_dp = lax.axis_size("fsdp"), lax.axis_size("dp")
    fsdp, dp = lax.axis_index("fsdp"), lax.axis_index("dp")
    top = n_dp // 2
    fsdp_at = fsdp.reshape(1)
    z_at = (dp // 2 % (top // 2)).reshape(1)
    four_at = (dp // top * 2 + dp % 2).reshape(1)
    swaps = [[(n, n ^ flip) for n in range(n_dp)] for flip in (1, top, top + 1)]
    up, down = (
        [(n, n // top * top + (n + 2 * way) % top) for n in range(n_dp)] for way in (1, -1)
    )

    x = residual.reshape(tokens, width)
    g = value_output_gradient.reshape(tokens, value_width)
    gain = input_norm_gain.reshape(width // 128, 128)
    chunk = width // n_fsdp

    refs_up = [lax.ppermute(reference_gradients, "dp", up)]
    refs_down = [lax.ppermute(reference_gradients, "dp", down)]

    weights = kernel(
        prep_kernel,
        "prep",
        shape((n_fsdp, 48, chunk), BF16),
        [SMEM] * 4 + [VMEM] * 3,
        vmem=FULL_MIB,
    )(fsdp_at, four_at, z_at, random_sketch_keys, gain, adapter_entry_matrix, adapter_exit_matrix)
    weights = lax.all_to_all(weights, "fsdp", 0, 0)

    early = kernel(
        early_kernel,
        "early",
        [shape((tokens, 128), F32)] * 2,
        [SMEM] + [HBM] * 2,
        [
            pltpu.VMEM((n_fsdp, tokens, chunk), BF16),
            pltpu.VMEM((width // 128, 128), F32),
            pltpu.VMEM((128, width), BF16),
            pltpu.SemaphoreType.DMA((1 + n_fsdp,)),
        ],
        vmem=FULL_MIB,
        flops=2 * tokens * width * 256,
        nbytes=12 * MIB,
    )(random_sketch_keys, gain, x)
    refs_up.append(lax.ppermute(refs_up[0], "dp", up))
    refs_down.append(lax.ppermute(refs_down[0], "dp", down))

    features = kernel(
        main_kernel,
        "features",
        shape((8, 128, 128), F32),
        [SMEM] * 3 + [HBM] * 6,
        [
            pltpu.VMEM((seq_count, local_len), I32),
            pltpu.VMEM((tokens, 128), F32),
            pltpu.VMEM((tokens, 128), F32),
            pltpu.VMEM((n_fsdp, 48, chunk), BF16),
            pltpu.VMEM((tokens, value_width), BF16),
            pltpu.VMEM((n_fsdp, tokens, chunk), BF16),
            pltpu.VMEM((8, 128, 128), F32),
            pltpu.VMEM((2, 96, tokens), F32),
            pltpu.VMEM((2, 512, tokens), BF16),
            pltpu.VMEM((2, 512, tokens), BF16),
            pltpu.SemaphoreType.DMA((5 + n_fsdp,)),
            pltpu.SemaphoreType.DMA((2,)),
        ],
        vmem=FULL_MIB,
        flops=2 * tokens * width * 256,
        nbytes=12 * MIB,
        outs=HBM,
    )(
        fsdp_at,
        random_sketch_keys,
        live_row_length,
        position_example_index,
        *early,
        weights,
        g,
        x,
    )
    refs_up.append(lax.ppermute(refs_up[1], "dp", up))
    refs_down.append(lax.ppermute(refs_down[1], "dp", down))
    features = lax.all_to_all(features, "fsdp", 0, 0)

    pieces = kernel(
        sum_kernel,
        "sum_features",
        [shape((16, 256), BF16)] * 4,
        [SMEM, VMEM],
        [pltpu.VMEM((4, 16, 256), BF16)],
    )(four_at, features)
    pieces = [pieces[0]] + [
        lax.ppermute(piece, "dp", swap) for piece, swap in zip(pieces[1:], swaps)
    ]
    feats = jnp.concatenate(pieces, axis=0)
    refs_up.append(lax.ppermute(refs_up[2], "dp", up))
    feats = jnp.broadcast_to(feats[None], (n_fsdp,) + feats.shape)
    feats = lax.all_to_all(feats, "fsdp", 0, 0)

    refs = [reference_gradients] + refs_up + refs_down[::-1]
    pieces = kernel(
        score_kernel,
        "partial_scores",
        [shape((16, 768), F32)] + [shape((16, 768), BF16)] * 3,
        [SMEM] + [VMEM] * 9,
        vmem=8,
    )(z_at, feats, *refs)
    pieces = [pieces[0]] + [
        lax.ppermute(piece, "dp", swap) for piece, swap in zip(pieces[1:], swaps)
    ]
    return kernel(
        final_kernel,
        "scores",
        shape((16, reference_gradients.shape[0]), F32),
        [VMEM] * 4,
    )(*pieces)


def solution(mesh):
    placed = (
        P("dp", "fsdp", None),
        P(),
        P("fsdp", None),
        P(None, "fsdp"),
        P("dp", "fsdp", None),
        P("dp", "fsdp"),
        P("dp"),
        P(),
        P("fsdp", "dp"),
    )
    return jax.shard_map(
        per_device, mesh=mesh, in_specs=placed, out_specs=P("dp", "fsdp"), check_vma=False
    )
```
